32 devices in a mesh: grp: 4 (over z), seq: 8 (over y, x, core).
Axes of the slice: x: 2, y: 2, z: 4, core: 2. Of those that a mesh axis runs over, the one named last changes fastest.
Arguments:
- queries: bfloat16 [128, 8192], P(('grp', 'seq')), may hold values from -200 to 200
- new_kv: bfloat16 [128, 2, 1024], P(('grp', 'seq')), may hold values from -8 to 8
- suffix_kv: bfloat16 [128, 2, 128, 1024], P(('grp', 'seq')), may hold values from -8 to 8
- suffix_len: int32 [128], P(('grp', 'seq')), may hold values from 1 to 128, 8192 in all
- prefix_of: int32 [128, 1], P(('grp', 'seq')), may hold values from 0 to 3; in each aligned block of 4 rows (0 to 3, 4 to 7, ...) at most 2 rows name the same one
- prefix_kv: bfloat16 [4, 2, 1024, 1024], P('grp', None, 'seq'), may hold values from -16 to 16
Outputs:
- attended: bfloat16 [128, 8192], P(('grp', 'seq'))
The draws below stay inside these ranges and needn't reach their ends.
Inputs may be any that keep to these rules, and one draw needn't show every extreme that they name: `prefix_of`: at most 2 of the 4 requests of one device name the same group, and that bound is reached on some device.
All inputs are finite; a program needn't handle non-finite values. No bound on the sum of `suffix_len` on one device may be relied on, other than what follows from the above.
Results may differ from the reference program's by a relative error of at most 0.0029.
Values may be sent and summed in bfloat16 or wider, within the bound.
No kernel may reach another device: no remote copies, remote signals or barrier semaphores. Data moves between devices by JAX's collectives and lax.ppermute only.
A program may use at most 128 MiB of HBM per device.

```python
import math
import jax
import jax.numpy as jnp
import numpy as np
from jax import lax

HEADS = 64
KVH = 8
HEAD = 128
REQ_DEV = 4
SUF = 128
CAP = 2
PREFIX = 1024
REQUESTS = 128
N_GRP = 4


def shared_keys(key):
    base_dir = jnp.clip(jax.random.normal(jax.random.fold_in(key, 901), (REQUESTS, KVH, HEAD), jnp.float32), -5.0, 5.0)
    spread = jnp.clip(jax.random.normal(jax.random.fold_in(key, 902), (REQUESTS, KVH, HEAD), jnp.float32), -5.0, 5.0)
    fresh = 0.6 * base_dir + spread
    return (base_dir, fresh)


def draw_queries(key, part):
    base_dir, fresh = shared_keys(key)
    key = jax.random.fold_in(key, 11)
    per_group = HEADS // KVH
    noise = jnp.clip(jax.random.normal(key, (REQUESTS, KVH, per_group, HEAD), jnp.float32), -5.0, 5.0)
    values = base_dir[:, :, None, :] + noise
    return values.reshape(REQUESTS, HEADS * HEAD).astype(jnp.bfloat16)


def draw_new_kv(key, part):
    base_dir, fresh = shared_keys(key)
    key = jax.random.fold_in(key, 12)
    values = jnp.clip(jax.random.normal(key, (REQUESTS, KVH * HEAD), jnp.float32), -5.0, 5.0)
    stacked = jnp.stack([fresh.reshape(REQUESTS, KVH * HEAD), values], axis=1)
    return stacked.astype(jnp.bfloat16)


def draw_suffix_kv(key, part):
    base_dir, fresh = shared_keys(key)
    key = jax.random.fold_in(key, 13)
    mix_key, noise_key, value_key = jax.random.split(key, 3)
    mixing = jax.random.uniform(mix_key, (REQUESTS, SUF, KVH, 1), jnp.float32, 0.2, 0.5)
    noise = jnp.clip(jax.random.normal(noise_key, (REQUESTS, SUF, KVH, HEAD), jnp.float32), -5.0, 5.0)
    values = jnp.clip(jax.random.normal(value_key, (REQUESTS, SUF, KVH * HEAD), jnp.float32), -5.0, 5.0)
    keys_all = mixing * base_dir[:, None, :, :] + noise
    stacked = jnp.stack([keys_all.reshape(REQUESTS, SUF, KVH * HEAD), values], axis=1)
    return stacked.astype(jnp.bfloat16)


def draw_prefix_kv(key, part):
    key = jax.random.fold_in(key, 14)
    scale_key, value_key, noise_key = jax.random.split(key, 3)
    key_scale = jnp.exp(jax.random.uniform(scale_key, (N_GRP, PREFIX, KVH, 1), jnp.float32, math.log(0.1), 0.0))
    value_scale = jnp.exp(jax.random.uniform(value_key, (N_GRP, PREFIX, KVH, 1), jnp.float32, math.log(0.3), math.log(3.0)))
    noise = jnp.clip(jax.random.normal(noise_key, (N_GRP, 2, PREFIX, KVH, HEAD), jnp.float32), -5.0, 5.0)
    key_part = noise[:, 0] * key_scale
    value_part = noise[:, 1] * value_scale
    stacked = jnp.stack([key_part, value_part], axis=1).reshape(N_GRP, 2, PREFIX, KVH * HEAD)
    return stacked.astype(jnp.bfloat16)


def profile(number_of, total, limit, skew):
    weights = [(1 << 20) // math.isqrt(grade ** skew) + 1 for grade in range(2, number_of + 1)]
    surplus, holding = total - limit - (number_of - 1), [1] * (number_of - 1)
    while surplus > 0:
        free = [i for i in range(number_of - 1) if holding[i] < limit]
        whole, left = sum([weights[i] for i in free]), surplus
        for i in free:
            extra = min(limit - holding[i], max(1, left * weights[i] // whole), surplus)
            holding[i] = holding[i] + extra
            surplus = surplus - extra
    return np.array([limit] + holding)


def uneven(rng, number_of, total, reach, skew):
    if number_of == 2:
        one = jax.random.randint(rng, (), max(1, total - reach), min(reach, total - 1) + 1)
        return jnp.stack([one, total - one])
    sizes = jnp.asarray(profile(number_of, total, reach, skew), jnp.int32)
    pairs = (number_of - 1) // 2
    giver, receiver = sizes[1:1 + 2 * pairs:2], sizes[2:2 + 2 * pairs:2]
    room = jnp.minimum(giver - 1, reach - receiver)
    moved = jax.random.randint(jax.random.fold_in(rng, 1), (pairs,), 0, 1 << 20) % (room + 1)
    sizes = sizes.at[1:1 + 2 * pairs:2].set(giver - moved).at[2:2 + 2 * pairs:2].set(receiver + moved)
    return sizes[jax.random.permutation(jax.random.fold_in(rng, 2), number_of)]


def deal_out(stream_key, own, number, rows, amount, top, bound, lean):
    order = jax.random.permutation(stream_key, amount)
    packed, usual = shares(amount, rows * top, bound, lean, True), shares(amount, rows * top, bound, lean, False)
    places = jnp.arange(amount)

    def named(lengths, offset_by):
        used = int((lengths > 0).sum())
        fixed = max(1, used // 4)
        shifted = fixed + (places - fixed + offset_by * (used - fixed)) % max(1, amount - fixed)
        return jnp.zeros((amount,), jnp.int32).at[order[jnp.where(places < fixed, places, shifted)]].set(jnp.asarray(lengths, jnp.int32))

    lengths = jnp.where(number % 4 == 0, named(packed, number // 4), named(usual, number - number // 4 - 1))
    mixed = jax.random.permutation(jax.random.fold_in(own, 3), amount)
    source_of, taker = mixed[0:amount // 2 * 2:2], mixed[1:amount // 2 * 2:2]
    slack = jnp.minimum(lengths[source_of] - 1, bound - lengths[taker]) // 2
    slack = jnp.where((source_of == order[0]) | (taker == order[0]) | (lengths[taker] == 0), 0, jnp.maximum(slack, 0))
    shifted = jax.random.randint(jax.random.fold_in(own, 4), (amount // 2,), 0, 1 << 20) % (slack + 1)
    lengths = lengths.at[source_of].add(-shifted).at[taker].add(shifted)
    members = jnp.searchsorted(jnp.cumsum(lengths), jnp.arange(rows * top), side="right").astype(jnp.int32)
    listing = members.reshape(top, rows).T
    listing = listing[jax.random.permutation(jax.random.fold_in(own, 1), rows)]
    offset_by = jax.random.randint(jax.random.fold_in(own, 2), (rows, 1), 0, top)
    return jnp.take_along_axis(listing, (jnp.arange(top)[None, :] + offset_by) % top, axis=1)


def shares(amount, total, reach, lean, full):
    weights = [(1 << 20) // math.isqrt(grade ** lean) + 1 for grade in range(1, amount + 1)]
    largest = reach if full else min(reach, max(-(-total // amount), total * weights[0] // sum(weights)))
    least = 1 if total - largest >= amount - 1 else 0
    holding, spare = [largest] + [least] * (amount - 1), total - largest - least * (amount - 1)
    while spare > 0:
        movable = [i for i in range(1, amount) if holding[i] < largest] or [i for i in range(1, amount) if holding[i] < reach]
        pool, left = sum([weights[i] for i in movable]), spare
        for i in movable:
            more = min(reach - holding[i], max(1, left * weights[i] // pool), spare)
            holding[i] = holding[i] + more
            spare = spare - more
    return np.array(holding)


def setup_inputs(seed: int = 0) -> dict:
    seeds = jax.random.split(jax.random.key(seed), 7)
    queries = draw_queries(jax.random.fold_in(seeds[6], 71), 0)
    new_kv = draw_new_kv(jax.random.fold_in(seeds[6], 71), 0)
    suffix_kv = draw_suffix_kv(jax.random.fold_in(seeds[6], 71), 0)
    suffix_len = uneven(seeds[3], REQUESTS, REQUESTS * SUF // 2, SUF, 2).astype(jnp.int32)
    prefix_of_keys = jax.random.split(jax.random.fold_in(seeds[4], 1), REQUESTS // REQ_DEV)
    prefix_of_turns = jax.random.permutation(jax.random.fold_in(seeds[4], 3), REQUESTS // REQ_DEV)
    prefix_of = jax.vmap(lambda own, number: deal_out(jax.random.fold_in(seeds[4], 2), own, number, REQ_DEV, N_GRP, 1, CAP, 2))(prefix_of_keys, prefix_of_turns).reshape((REQUESTS, 1))
    prefix_kv = draw_prefix_kv(jax.random.fold_in(seeds[6], 71), 0)
    return dict(queries=queries, new_kv=new_kv, suffix_kv=suffix_kv, suffix_len=suffix_len, prefix_of=prefix_of, prefix_kv=prefix_kv)


def rounded(values):
    return lax.optimization_barrier(values.astype(jnp.bfloat16)).astype(jnp.float32)


def reference(queries, new_kv, suffix_kv, suffix_len, prefix_of, prefix_kv):
    per_group = HEADS // KVH
    width_all = HEADS * HEAD
    score_scale = HEAD ** -0.5
    block_rows = 32
    routes = prefix_of[:, 0].astype(jnp.int32)
    order = jnp.argsort(routes, stable=True).astype(jnp.int32)
    group_ids = jnp.arange(N_GRP, dtype=jnp.int32)
    counts = jnp.sum((routes[None, :] == group_ids[:, None]).astype(jnp.int32), axis=1)
    starts = (jnp.cumsum(counts) - counts).astype(jnp.int32)
    block_count = ((counts + block_rows - 1) // block_rows).astype(jnp.int32)
    block_ends = jnp.cumsum(block_count).astype(jnp.int32)
    total_blocks = REQUESTS // block_rows + N_GRP
    padded_order = jnp.concatenate([order, jnp.zeros((block_rows,), jnp.int32)])
    sorted_queries = jnp.concatenate([queries[order], jnp.zeros((block_rows, width_all), queries.dtype)])

    def one_block(block_id):
        owner = jnp.sum((block_ends <= block_id).astype(jnp.int32))
        valid = owner < N_GRP
        owner_kept = jnp.minimum(owner, N_GRP - 1).astype(jnp.int32)
        first_block = block_ends[owner_kept] - block_count[owner_kept]
        row_start = starts[owner_kept] + block_rows * (block_id - first_block)
        row_start = jnp.where(valid, row_start, 0).astype(jnp.int32)
        row_ids = row_start + jnp.arange(block_rows, dtype=jnp.int32)
        live_rows = valid & (row_ids < starts[owner_kept] + counts[owner_kept])
        target = jnp.where(live_rows, padded_order[row_ids], REQUESTS).astype(jnp.int32)
        query_block = lax.dynamic_slice_in_dim(sorted_queries, row_start, block_rows, 0)
        query_block = query_block.astype(jnp.float32).reshape(block_rows, KVH, per_group, HEAD)
        cache = lax.dynamic_index_in_dim(prefix_kv, owner_kept, 0, keepdims=False).astype(jnp.float32)
        key_rows = cache[0].reshape(PREFIX, KVH, HEAD)
        value_rows = cache[1].reshape(PREFIX, KVH, HEAD)
        scores = jnp.einsum("bkgd,tkd->bkgt", query_block, key_rows) * score_scale
        top_score = jnp.max(scores, axis=3)
        expo_terms = jnp.exp(scores - top_score[..., None])
        partial_value = jnp.einsum("bkgt,tkd->bkgd", rounded(expo_terms), value_rows)
        return (partial_value.reshape(block_rows, width_all), jnp.sum(expo_terms, axis=3).reshape(block_rows, HEADS),
                top_score.reshape(block_rows, HEADS), target)

    partials, totals, maxima, targets = lax.map(one_block, jnp.arange(total_blocks, dtype=jnp.int32))
    flat_targets = targets.reshape(-1)
    prefix_out = jnp.zeros((REQUESTS, width_all), jnp.float32).at[flat_targets].set(partials.reshape(-1, width_all), mode="drop")
    prefix_total = jnp.zeros((REQUESTS, HEADS), jnp.float32).at[flat_targets].set(totals.reshape(-1, HEADS), mode="drop")
    prefix_max = jnp.zeros((REQUESTS, HEADS), jnp.float32).at[flat_targets].set(maxima.reshape(-1, HEADS), mode="drop")

    suffix_block = 64 if REQUESTS % 64 == 0 else 32
    suffix_blocks = REQUESTS // suffix_block

    def suffix_part(inputs):
        query_block, fresh_block, cache_block, length_block = inputs
        query_heads = query_block.astype(jnp.float32).reshape(suffix_block, KVH, per_group, HEAD)
        suffix_keys = cache_block[:, 0].astype(jnp.float32).reshape(suffix_block, SUF, KVH, HEAD)
        suffix_values = cache_block[:, 1].astype(jnp.float32).reshape(suffix_block, SUF, KVH, HEAD)
        own_key = fresh_block[:, 0].astype(jnp.float32).reshape(suffix_block, KVH, HEAD)
        own_value = fresh_block[:, 1].astype(jnp.float32).reshape(suffix_block, KVH, HEAD)
        scores = jnp.einsum("rkgd,rtkd->rkgt", query_heads, suffix_keys) * score_scale
        live_keys = jnp.arange(SUF, dtype=jnp.int32)[None, :] < length_block[:, None]
        scores = jnp.where(live_keys[:, None, None, :], scores, -jnp.inf)
        own_score = jnp.einsum("rkgd,rkd->rkg", query_heads, own_key) * score_scale
        suffix_max = jnp.maximum(jnp.max(scores, axis=3), own_score)
        expo_terms = jnp.exp(scores - suffix_max[..., None])
        own_expo = jnp.exp(own_score - suffix_max)
        suffix_out = jnp.einsum("rkgt,rtkd->rkgd", rounded(expo_terms), suffix_values)
        suffix_out = suffix_out + rounded(own_expo)[..., None] * own_value[:, :, None, :]
        suffix_total = jnp.sum(expo_terms, axis=3) + own_expo
        return (suffix_out.reshape(suffix_block, HEADS, HEAD), suffix_max.reshape(suffix_block, HEADS),
                suffix_total.reshape(suffix_block, HEADS))

    suffix_out, suffix_max, suffix_total = lax.map(suffix_part, (
        queries.reshape(suffix_blocks, suffix_block, width_all),
        new_kv.reshape(suffix_blocks, suffix_block, 2, KVH * HEAD),
        suffix_kv.reshape(suffix_blocks, suffix_block, 2, SUF, KVH * HEAD),
        suffix_len.reshape(suffix_blocks, suffix_block)))
    suffix_out = suffix_out.reshape(REQUESTS, HEADS, HEAD)
    suffix_max = suffix_max.reshape(REQUESTS, HEADS)
    suffix_total = suffix_total.reshape(REQUESTS, HEADS)

    top_all = jnp.maximum(prefix_max, suffix_max)
    from_prefix = jnp.exp(prefix_max - top_all)
    from_suffix = jnp.exp(suffix_max - top_all)
    numer = from_prefix[..., None] * prefix_out.reshape(REQUESTS, HEADS, HEAD) + from_suffix[..., None] * suffix_out
    denom = from_prefix * prefix_total + from_suffix * suffix_total
    return (numer / denom[..., None]).reshape(REQUESTS, width_all).astype(jnp.bfloat16)
```

```python
import functools
import math

import jax
import jax.numpy as jnp
from jax import lax
from jax.experimental import pallas as pl
from jax.experimental.pallas import tpu as pltpu
from jax.sharding import PartitionSpec as P

HEADS = 64
KVH = 8
HEAD = 128
CAP = 2
PER = HEADS // KVH
SCALE = HEAD ** (-0.5)
LOG2E = math.log2(math.e)
LN2 = math.log(2.0)
SEND = jnp.bfloat16
ROWS = CAP * PER
BACK = ROWS + PER
NT = (((1,), (1,)), ((), ()))
VMEM = pl.BlockSpec(memory_space=pltpu.VMEM)
SMEM = pl.BlockSpec(memory_space=pltpu.SMEM)
ANY = pl.BlockSpec(memory_space=pl.ANY)


def slots_of(routes_ref, requests):
    routes = [routes_ref[r, 0] for r in range(requests)]
    ranks = []
    for r in range(requests):
        rank = jnp.int32(0)
        for e in range(r):
            rank = rank + jnp.where(routes[e] == routes[r], 1, 0)
        ranks.append(rank)
    return routes, ranks


def pack_queries(groups, splits, routes_ref, q_ref, out_ref, rows_ref, x_ref):
    requests = q_ref.shape[0]
    routes, ranks = slots_of(routes_ref, requests)
    q = q_ref[...].astype(jnp.float32)
    for k in range(KVH):
        for h in range(PER):
            x_ref[h * requests:(h + 1) * requests, k * HEAD:(k + 1) * HEAD] = q[
                :, (k * PER + h) * HEAD:(k * PER + h + 1) * HEAD
            ]
    x = x_ref[...].astype(jnp.bfloat16)
    cols = PER * requests
    total = groups * ROWS
    row = lax.broadcasted_iota(jnp.int32, (total, cols), 0)
    col = lax.broadcasted_iota(jnp.int32, (total, cols), 1)
    wanted = jnp.full((total, cols), -1, jnp.int32)
    for r in range(requests):
        wanted = jnp.where(col % requests == r, routes[r] * CAP + ranks[r], wanted)
    pick = (row // PER == wanted) & (row % PER == col // requests)
    placed = jnp.dot(
        pick.astype(jnp.float32).astype(jnp.bfloat16), x, preferred_element_type=jnp.float32
    ).astype(jnp.bfloat16)
    for g in range(groups):
        for k in range(KVH):
            tile = placed[g * ROWS:(g + 1) * ROWS, k * HEAD:(k + 1) * HEAD]
            for t in range(splits):
                out_ref[g, t, k] = tile
    mine = requests * PER
    row = lax.broadcasted_iota(jnp.int32, (mine, cols), 0)
    col = lax.broadcasted_iota(jnp.int32, (mine, cols), 1)
    turn = (row // PER == col % requests) & (row % PER == col // requests)
    turned = jnp.dot(
        turn.astype(jnp.float32).astype(jnp.bfloat16), x, preferred_element_type=jnp.float32
    )
    for r in range(requests):
        for k in range(KVH):
            rows_ref[r, k * PER:(k + 1) * PER, :] = turned[
                r * PER:(r + 1) * PER, k * HEAD:(k + 1) * HEAD
            ]


def split_heads(kv_ref, *refs):
    outs, sems = refs[:-1], refs[-1]
    mine = lax.axis_index("seq") % KVH
    copies = []
    for j in range(KVH):
        head = jnp.bitwise_xor(mine, j)
        start = pl.multiple_of(head * HEAD, HEAD)
        copies.append(
            pltpu.make_async_copy(kv_ref.at[0, :, :, pl.ds(start, HEAD)], outs[j], sems.at[j])
        )
    for copy in copies:
        copy.start()
    for copy in copies:
        copy.wait()


def suffix_kernel(len_ref, rows_ref, new_ref, kv_ref, out_ref, stat_ref):
    r = pl.program_id(0)
    span = kv_ref.shape[2]
    q = rows_ref[0]
    new = new_ref[pl.ds(r, 1)][0].astype(jnp.float32)
    zero = jnp.zeros((PER, HEAD), jnp.float32)
    wide = jnp.concatenate(
        [
            jnp.concatenate(
                [q[k * PER:(k + 1) * PER] if j == k else zero for j in range(KVH)], axis=1
            )
            for k in range(KVH)
        ],
        axis=0,
    ).astype(jnp.bfloat16)
    raw = lax.dot_general(wide, kv_ref[0, 0], NT, preferred_element_type=jnp.float32)
    live = lax.broadcasted_iota(jnp.int32, raw.shape, 1) < len_ref[r]
    raw = jnp.where(live, raw, -jnp.inf)
    own = jnp.concatenate(
        [
            jnp.sum(
                q[k * PER:(k + 1) * PER] * new[0:1, k * HEAD:(k + 1) * HEAD],
                axis=1,
                keepdims=True,
            )
            for k in range(KVH)
        ],
        axis=0,
    )
    top = jnp.maximum(jnp.max(raw, axis=1, keepdims=True), own)
    weight = jnp.exp2((raw - top) * (SCALE * LOG2E))
    own_weight = jnp.exp2((own - top) * (SCALE * LOG2E))
    total = jnp.sum(weight, axis=1, keepdims=True) + own_weight
    full = jnp.dot(weight.astype(jnp.bfloat16), kv_ref[0, 1], preferred_element_type=jnp.float32)
    own_rounded = own_weight.astype(jnp.bfloat16).astype(jnp.float32)
    for k in range(KVH):
        rows = slice(k * PER, (k + 1) * PER)
        cols = slice(k * HEAD, (k + 1) * HEAD)
        out_ref[0, rows, :] = full[rows, cols] + own_rounded[rows] * new[1:2, cols]
    lane = lax.broadcasted_iota(jnp.int32, (HEADS, HEAD), 1)
    stat_ref[0] = jnp.where(lane == 0, top * SCALE, total)


def prefix_kernel(q_ref, *refs):
    parts, out_ref = refs[:-1], refs[-1]
    keys = jnp.concatenate([part[0] for part in parts], axis=0)
    values = jnp.concatenate([part[1] for part in parts], axis=0)
    sources = q_ref.shape[0]
    step = 8
    lane = lax.broadcasted_iota(jnp.int32, (step * ROWS, HEAD), 1)

    def block(i):
        q = q_ref[pl.ds(i * step, step)].reshape(step * ROWS, HEAD)
        raw = lax.dot_general(q, keys, NT, preferred_element_type=jnp.float32)
        top = jnp.max(raw, axis=1, keepdims=True)
        weight = jnp.exp2((raw - top) * (SCALE * LOG2E))
        total = jnp.sum(weight, axis=1, keepdims=True)
        out = jnp.dot(weight.astype(jnp.bfloat16), values, preferred_element_type=jnp.float32)
        out = (out / total).astype(SEND)
        level = top * SCALE + jnp.log(total)
        first = level.astype(SEND).astype(jnp.float32)
        rest = level - first
        second = rest.astype(SEND).astype(jnp.float32)
        third = rest - second
        stat = jnp.where(
            lane == 0, first, jnp.where(lane == 1, second, jnp.where(lane == 2, third, 0.0))
        )
        for s in range(step):
            at = i * step + s
            out_ref[at, 0:ROWS, :] = out[s * ROWS:(s + 1) * ROWS]
            two = stat[s * ROWS:(s + 1) * ROWS]
            joined = two[0:PER]
            for c in range(1, CAP):
                joined = joined + pltpu.roll(two[c * PER:(c + 1) * PER], c * (HEAD // CAP), 1)
            out_ref[at, ROWS:BACK, :] = joined.astype(SEND)

    if sources // step <= 4:
        for i in range(sources // step):
            block(i)
    else:
        lax.fori_loop(0, sources // step, lambda i, c: (block(i), c)[1], 0)


def join_kernel(splits, routes_ref, back_ref, suffix_ref, stat_ref, out_ref):
    requests = out_ref.shape[0]
    routes, ranks = slots_of(routes_ref, requests)
    lane = lax.broadcasted_iota(jnp.int32, (PER, HEAD), 1) // (HEAD // CAP)
    pieces = [[None] * requests for _ in range(KVH)]
    for r in range(requests):
        stats = stat_ref[r]
        for k in range(KVH):
            rows = slice(k * PER, (k + 1) * PER)
            levels, parts = [], []
            for t in range(splits):
                both = back_ref[routes[r], t, k, 0:ROWS, :].astype(jnp.float32)
                part = both[0:PER]
                for c in range(1, CAP):
                    part = jnp.where(ranks[r] == c, both[c * PER:(c + 1) * PER], part)
                parts.append(part)
                stat = back_ref[routes[r], t, k, ROWS:BACK, :].astype(jnp.float32)
                levels.append(
                    jnp.sum(jnp.where(lane == ranks[r], stat, 0.0), axis=1, keepdims=True)
                )
            suffix_top = stats[rows, 0:1]
            top = suffix_top
            for level in levels:
                top = jnp.maximum(top, level)
            from_suffix = jnp.exp(suffix_top - top)
            numer = from_suffix * suffix_ref[r, rows, :]
            denom = from_suffix * stats[rows, 1:2]
            for level, part in zip(levels, parts):
                from_prefix = jnp.exp(level - top)
                numer = numer + from_prefix * part
                denom = denom + from_prefix
            pieces[k][r] = numer / denom
    stacked = jnp.concatenate(
        [jnp.concatenate(pieces[k], axis=0) for k in range(KVH)], axis=1
    ).astype(jnp.bfloat16)
    mine = requests * PER
    row = lax.broadcasted_iota(jnp.int32, (PER * 8, mine), 0)
    col = lax.broadcasted_iota(jnp.int32, (PER * 8, mine), 1)
    turn = (row % 8 == col // PER) & (row // 8 == col % PER)
    turned = jnp.dot(
        turn.astype(jnp.float32).astype(jnp.bfloat16), stacked, preferred_element_type=jnp.float32
    ).astype(jnp.bfloat16)
    turned = turned.astype(jnp.float32)
    for k in range(KVH):
        for h in range(PER):
            out_ref[:, (k * PER + h) * HEAD:(k * PER + h + 1) * HEAD] = turned[
                h * 8:h * 8 + requests, k * HEAD:(k + 1) * HEAD
            ].astype(jnp.bfloat16)


def on_device(queries, new_kv, suffix_kv, suffix_len, prefix_of, prefix_kv):
    groups = lax.axis_size("grp")
    seq = lax.axis_size("seq")
    splits = seq // KVH
    requests = queries.shape[0]
    span = suffix_kv.shape[2]
    here = prefix_kv.shape[2]
    everyone = ("grp", "seq")

    outgoing, rows = pl.pallas_call(
        functools.partial(pack_queries, groups, splits),
        out_shape=(
            jax.ShapeDtypeStruct((groups, splits, KVH, ROWS, HEAD), jnp.bfloat16),
            jax.ShapeDtypeStruct((requests, HEADS, HEAD), jnp.float32),
        ),
        in_specs=[SMEM, VMEM],
        out_specs=(VMEM, VMEM),
        scratch_shapes=[pltpu.VMEM((PER * requests, KVH * HEAD), jnp.float32)],
        name="pack_queries",
    )(prefix_of, queries)

    blocks = pl.pallas_call(
        split_heads,
        out_shape=[jax.ShapeDtypeStruct((2, here, HEAD), jnp.bfloat16)] * KVH,
        in_specs=[ANY],
        out_specs=[ANY] * KVH,
        scratch_shapes=[pltpu.SemaphoreType.DMA((KVH,))],
        name="split_heads",
    )(prefix_kv)
    parts = [blocks[0]]
    for j in range(1, KVH):
        parts.append(lax.ppermute(blocks[j], "seq", [(s, s ^ j) for s in range(seq)]))

    arrived = lax.all_to_all(
        outgoing.reshape(groups * seq, ROWS, HEAD), everyone, split_axis=0, concat_axis=0, tiled=True
    )

    suffix_out, suffix_stat = pl.pallas_call(
        suffix_kernel,
        grid=(requests,),
        out_shape=(
            jax.ShapeDtypeStruct((requests, HEADS, HEAD), jnp.float32),
            jax.ShapeDtypeStruct((requests, HEADS, HEAD), jnp.float32),
        ),
        in_specs=[
            SMEM,
            pl.BlockSpec((1, HEADS, HEAD), lambda r: (r, 0, 0)),
            pl.BlockSpec((requests, 2, KVH * HEAD), lambda r: (0, 0, 0)),
            pl.BlockSpec((1, 2, span, KVH * HEAD), lambda r: (r, 0, 0, 0)),
        ],
        out_specs=(
            pl.BlockSpec((1, HEADS, HEAD), lambda r: (r, 0, 0)),
            pl.BlockSpec((1, HEADS, HEAD), lambda r: (r, 0, 0)),
        ),
        cost_estimate=pl.CostEstimate(
            flops=4 * requests * HEADS * KVH * HEAD * span,
            bytes_accessed=2 * suffix_kv.size,
            transcendentals=requests * HEADS * span,
        ),
        name="suffix_attention",
    )(suffix_len, rows, new_kv, suffix_kv)

    back = pl.pallas_call(
        prefix_kernel,
        out_shape=jax.ShapeDtypeStruct((groups * seq, BACK, HEAD), SEND),
        in_specs=[VMEM] * (1 + KVH),
        out_specs=VMEM,
        compiler_params=pltpu.CompilerParams(vmem_limit_bytes=32 * 1024 * 1024),
        name="prefix_attention",
    )(arrived, *parts)

    home = lax.all_to_all(back, everyone, split_axis=0, concat_axis=0, tiled=True)

    return pl.pallas_call(
        functools.partial(join_kernel, splits),
        out_shape=jax.ShapeDtypeStruct((requests, HEADS * HEAD), jnp.bfloat16),
        in_specs=[SMEM, VMEM, VMEM, VMEM],
        out_specs=VMEM,
        name="join",
    )(prefix_of, home.reshape(groups, splits, KVH, BACK, HEAD), suffix_out, suffix_stat)


def solution(mesh):
    in_specs = (
        P(("grp", "seq"), None),
        P(("grp", "seq"), None, None),
        P(("grp", "seq"), None, None, None),
        P(("grp", "seq")),
        P(("grp", "seq"), None),
        P("grp", None, "seq", None),
    )
    out_specs = P(("grp", "seq"), None)
    return jax.shard_map(
        on_device, mesh=mesh, in_specs=in_specs, out_specs=out_specs, check_vma=False
    )
```

```python
import functools
import math

import jax
import jax.numpy as jnp
from jax import lax
from jax.experimental import pallas as pl
from jax.experimental.pallas import tpu as pltpu
from jax.sharding import PartitionSpec as P

HEADS = 64
KVH = 8
HEAD = 128
CAP = 2
PER = HEADS // KVH
SCALE = HEAD ** (-0.5)
LOG2E = math.log2(math.e)
LN2 = math.log(2.0)
SEND = jnp.bfloat16
ROWS = CAP * PER
BACK = ROWS + PER
NT = (((1,), (1,)), ((), ()))
VMEM = pl.BlockSpec(memory_space=pltpu.VMEM)
SMEM = pl.BlockSpec(memory_space=pltpu.SMEM)
ANY = pl.BlockSpec(memory_space=pl.ANY)


def slots_of(routes_ref, requests):
    routes = [routes_ref[r] for r in range(requests)]
    ranks = []
    for r in range(requests):
        rank = jnp.int32(0)
        for e in range(r):
            rank = rank + jnp.where(routes[e] == routes[r], 1, 0)
        ranks.append(rank)
    return routes, ranks


def pack_queries(groups, splits, routes_ref, q_ref, out_ref, rows_ref, x_ref):
    requests = q_ref.shape[0]
    routes, ranks = slots_of(routes_ref, requests)
    q = q_ref[...].astype(jnp.float32)
    for k in range(KVH):
        for h in range(PER):
            x_ref[h * requests:(h + 1) * requests, k * HEAD:(k + 1) * HEAD] = q[
                :, (k * PER + h) * HEAD:(k * PER + h + 1) * HEAD
            ]
    x = x_ref[...].astype(jnp.bfloat16)
    cols = PER * requests
    total = groups * ROWS
    row = lax.broadcasted_iota(jnp.int32, (total, cols), 0)
    col = lax.broadcasted_iota(jnp.int32, (total, cols), 1)
    wanted = jnp.full((total, cols), -1, jnp.int32)
    for r in range(requests):
        wanted = jnp.where(col % requests == r, routes[r] * CAP + ranks[r], wanted)
    pick = (row // PER == wanted) & (row % PER == col // requests)
    placed = jnp.dot(
        pick.astype(jnp.float32).astype(jnp.bfloat16), x, preferred_element_type=jnp.float32
    ).astype(jnp.bfloat16)
    for g in range(groups):
        for k in range(KVH):
            tile = placed[g * ROWS:(g + 1) * ROWS, k * HEAD:(k + 1) * HEAD]
            for t in range(splits):
                out_ref[g, t, k] = tile
    mine = requests * PER
    row = lax.broadcasted_iota(jnp.int32, (mine, cols), 0)
    col = lax.broadcasted_iota(jnp.int32, (mine, cols), 1)
    turn = (row // PER == col % requests) & (row % PER == col // requests)
    turned = jnp.dot(
        turn.astype(jnp.float32).astype(jnp.bfloat16), x, preferred_element_type=jnp.float32
    )
    for r in range(requests):
        for k in range(KVH):
            rows_ref[r, k * PER:(k + 1) * PER, :] = turned[
                r * PER:(r + 1) * PER, k * HEAD:(k + 1) * HEAD
            ]


def prepare(groups, splits, routes_ref, q_ref, kv_ref, out_ref, rows_ref, *refs):
    blocks, (x_ref, sems) = refs[:KVH], refs[KVH:]
    mine = lax.axis_index("seq") % KVH
    copies = []
    for j in range(KVH):
        start = pl.multiple_of(jnp.bitwise_xor(mine, j) * HEAD, HEAD)
        copies.append(
            pltpu.make_async_copy(kv_ref.at[0, :, :, pl.ds(start, HEAD)], blocks[j], sems.at[j])
        )
    for copy in copies:
        copy.start()
    pack_queries(groups, splits, routes_ref, q_ref, out_ref, rows_ref, x_ref)
    for copy in copies:
        copy.wait()


def suffix_kernel(len_ref, rows_ref, new_ref, kv_ref, out_ref, stat_ref):
    requests = rows_ref.shape[0]
    zero = jnp.zeros((PER, HEAD), jnp.float32)
    lane = lax.broadcasted_iota(jnp.int32, (HEADS, HEAD), 1)
    for r in range(requests):
        q = rows_ref[r]
        new = new_ref[r].astype(jnp.float32)
        wide = jnp.concatenate(
            [
                jnp.concatenate(
                    [q[k * PER:(k + 1) * PER] if j == k else zero for j in range(KVH)], axis=1
                )
                for k in range(KVH)
            ],
            axis=0,
        ).astype(jnp.bfloat16)
        raw = lax.dot_general(wide, kv_ref[r, 0], NT, preferred_element_type=jnp.float32)
        live = lax.broadcasted_iota(jnp.int32, raw.shape, 1) < len_ref[r]
        raw = jnp.where(live, raw, -jnp.inf)
        own = jnp.concatenate(
            [
                jnp.sum(
                    q[k * PER:(k + 1) * PER] * new[0:1, k * HEAD:(k + 1) * HEAD],
                    axis=1,
                    keepdims=True,
                )
                for k in range(KVH)
            ],
            axis=0,
        )
        top = jnp.maximum(jnp.max(raw, axis=1, keepdims=True), own)
        weight = jnp.exp2((raw - top) * (SCALE * LOG2E))
        own_weight = jnp.exp2((own - top) * (SCALE * LOG2E))
        total = jnp.sum(weight, axis=1, keepdims=True) + own_weight
        full = jnp.dot(
            weight.astype(jnp.bfloat16), kv_ref[r, 1], preferred_element_type=jnp.float32
        )
        own_rounded = own_weight.astype(jnp.bfloat16).astype(jnp.float32)
        for k in range(KVH):
            rows = slice(k * PER, (k + 1) * PER)
            cols = slice(k * HEAD, (k + 1) * HEAD)
            out_ref[r, rows, :] = full[rows, cols] + own_rounded[rows] * new[1:2, cols]
        stat_ref[r] = jnp.where(lane == 0, top * SCALE, total)


def prefix_kernel(q_ref, own_ref, *refs):
    parts, (out_ref, own, sem) = refs[:-3], refs[-3:]
    copy = pltpu.make_async_copy(own_ref, own, sem)
    copy.start()
    copy.wait()
    keys = jnp.concatenate([part[0] for part in parts] + [own[0]], axis=0)
    values = jnp.concatenate([part[1] for part in parts] + [own[1]], axis=0)
    sources = q_ref.shape[0]
    step = 8
    lane = lax.broadcasted_iota(jnp.int32, (step * ROWS, HEAD), 1)

    def block(i):
        q = q_ref[pl.ds(i * step, step)].reshape(step * ROWS, HEAD)
        raw = lax.dot_general(q, keys, NT, preferred_element_type=jnp.float32)
        top = jnp.max(raw, axis=1, keepdims=True)
        weight = jnp.exp2((raw - top) * (SCALE * LOG2E))
        total = jnp.sum(weight, axis=1, keepdims=True)
        out = jnp.dot(weight.astype(jnp.bfloat16), values, preferred_element_type=jnp.float32)
        out = (out / total).astype(SEND)
        level = top * SCALE + jnp.log(total)
        first = level.astype(SEND).astype(jnp.float32)
        rest = level - first
        second = rest.astype(SEND).astype(jnp.float32)
        third = rest - second
        stat = jnp.where(
            lane == 0, first, jnp.where(lane == 1, second, jnp.where(lane == 2, third, 0.0))
        )
        for s in range(step):
            at = i * step + s
            out_ref[at, 0:ROWS, :] = out[s * ROWS:(s + 1) * ROWS]
            two = stat[s * ROWS:(s + 1) * ROWS]
            joined = two[0:PER]
            for c in range(1, CAP):
                joined = joined + pltpu.roll(two[c * PER:(c + 1) * PER], c * (HEAD // CAP), 1)
            out_ref[at, ROWS:BACK, :] = joined.astype(SEND)

    if sources // step <= 4:
        for i in range(sources // step):
            block(i)
    else:
        lax.fori_loop(0, sources // step, lambda i, c: (block(i), c)[1], 0)


def join_kernel(splits, routes_ref, back_ref, suffix_ref, stat_ref, out_ref):
    requests = out_ref.shape[0]
    routes, ranks = slots_of(routes_ref, requests)
    lane = lax.broadcasted_iota(jnp.int32, (PER, HEAD), 1) // (HEAD // CAP)
    pieces = [[None] * requests for _ in range(KVH)]
    for r in range(requests):
        stats = stat_ref[r]
        for k in range(KVH):
            rows = slice(k * PER, (k + 1) * PER)
            levels, parts = [], []
            for t in range(splits):
                at = (routes[r] * splits + t) * KVH + k
                both = back_ref[at, 0:ROWS, :].astype(jnp.float32)
                part = both[0:PER]
                for c in range(1, CAP):
                    part = jnp.where(ranks[r] == c, both[c * PER:(c + 1) * PER], part)
                parts.append(part)
                stat = back_ref[at, ROWS:BACK, :].astype(jnp.float32)
                levels.append(
                    jnp.sum(jnp.where(lane == ranks[r], stat, 0.0), axis=1, keepdims=True)
                )
            suffix_top = stats[rows, 0:1]
            top = suffix_top
            for level in levels:
                top = jnp.maximum(top, level)
            from_suffix = jnp.exp(suffix_top - top)
            numer = from_suffix * suffix_ref[r, rows, :]
            denom = from_suffix * stats[rows, 1:2]
            for level, part in zip(levels, parts):
                from_prefix = jnp.exp(level - top)
                numer = numer + from_prefix * part
                denom = denom + from_prefix
            pieces[k][r] = numer / denom
    stacked = jnp.concatenate(
        [jnp.concatenate(pieces[k], axis=0) for k in range(KVH)], axis=1
    ).astype(jnp.bfloat16)
    mine = requests * PER
    row = lax.broadcasted_iota(jnp.int32, (PER * 8, mine), 0)
    col = lax.broadcasted_iota(jnp.int32, (PER * 8, mine), 1)
    turn = (row % 8 == col // PER) & (row // 8 == col % PER)
    turned = jnp.dot(
        turn.astype(jnp.float32).astype(jnp.bfloat16), stacked, preferred_element_type=jnp.float32
    ).astype(jnp.bfloat16)
    turned = turned.astype(jnp.float32)
    for k in range(KVH):
        for h in range(PER):
            out_ref[:, (k * PER + h) * HEAD:(k * PER + h + 1) * HEAD] = turned[
                h * 8:h * 8 + requests, k * HEAD:(k + 1) * HEAD
            ].astype(jnp.bfloat16)


def on_device(queries, new_kv, suffix_kv, suffix_len, prefix_of, prefix_kv):
    groups = lax.axis_size("grp")
    seq = lax.axis_size("seq")
    splits = seq // KVH
    requests = queries.shape[0]
    span = suffix_kv.shape[2]
    here = prefix_kv.shape[2]
    everyone = ("grp", "seq")
    routes = prefix_of.reshape(requests)

    outgoing, rows, *blocks = pl.pallas_call(
        functools.partial(prepare, groups, splits),
        out_shape=[
            jax.ShapeDtypeStruct((groups, splits, KVH, ROWS, HEAD), jnp.bfloat16),
            jax.ShapeDtypeStruct((requests, HEADS, HEAD), jnp.float32),
        ]
        + [jax.ShapeDtypeStruct((2, here, HEAD), jnp.bfloat16)] * KVH,
        in_specs=[SMEM, VMEM, ANY],
        out_specs=[VMEM] * (2 + KVH),
        scratch_shapes=[
            pltpu.VMEM((PER * requests, KVH * HEAD), jnp.float32),
            pltpu.SemaphoreType.DMA((KVH,)),
        ],
        name="prepare",
    )(routes, queries, prefix_kv)
    parts = [blocks[0]]
    for j in range(1, KVH):
        parts.append(lax.ppermute(blocks[j], "seq", [(s, s ^ j) for s in range(seq)]))

    arrived = lax.all_to_all(
        outgoing.reshape(groups * seq, ROWS, HEAD), everyone, split_axis=0, concat_axis=0, tiled=True
    )

    suffix_out, suffix_stat = pl.pallas_call(
        suffix_kernel,
        out_shape=(
            jax.ShapeDtypeStruct((requests, HEADS, HEAD), jnp.float32),
            jax.ShapeDtypeStruct((requests, HEADS, HEAD), jnp.float32),
        ),
        in_specs=[SMEM, VMEM, VMEM, VMEM],
        out_specs=(VMEM, VMEM),
        cost_estimate=pl.CostEstimate(
            flops=4 * requests * HEADS * KVH * HEAD * span,
            bytes_accessed=2 * suffix_kv.size,
            transcendentals=requests * HEADS * span,
        ),
        name="suffix_attention",
    )(suffix_len, rows, new_kv, suffix_kv)

    arrived, suffix_out, suffix_stat = lax.optimization_barrier(
        (arrived, suffix_out, suffix_stat)
    )

    back = pl.pallas_call(
        prefix_kernel,
        out_shape=jax.ShapeDtypeStruct((groups * seq, BACK, HEAD), SEND),
        in_specs=[VMEM, ANY] + [VMEM] * (KVH - 1),
        out_specs=VMEM,
        scratch_shapes=[
            pltpu.VMEM((2, here, HEAD), jnp.bfloat16),
            pltpu.SemaphoreType.DMA,
        ],
        compiler_params=pltpu.CompilerParams(vmem_limit_bytes=32 * 1024 * 1024),
        name="prefix_attention",
    )(arrived, *parts)

    home = lax.all_to_all(back, everyone, split_axis=0, concat_axis=0, tiled=True)

    return pl.pallas_call(
        functools.partial(join_kernel, splits),
        out_shape=jax.ShapeDtypeStruct((requests, HEADS * HEAD), jnp.bfloat16),
        in_specs=[SMEM, VMEM, VMEM, VMEM],
        out_specs=VMEM,
        name="join",
    )(routes, home, suffix_out, suffix_stat)


def solution(mesh):
    in_specs = (
        P(("grp", "seq"), None),
        P(("grp", "seq"), None, None),
        P(("grp", "seq"), None, None, None),
        P(("grp", "seq")),
        P(("grp", "seq"), None),
        P("grp", None, "seq", None),
    )
    out_specs = P(("grp", "seq"), None)
    return jax.shard_map(
        on_device, mesh=mesh, in_specs=in_specs, out_specs=out_specs, check_vma=False
    )
```

```python
import functools
import math

import jax
import jax.numpy as jnp
from jax import lax
from jax.experimental import pallas as pl
from jax.experimental.pallas import tpu as pltpu
from jax.sharding import PartitionSpec as P

HEADS = 64
KVH = 8
HEAD = 128
CAP = 2
PER = HEADS // KVH
SCALE = HEAD ** (-0.5)
LOG2E = math.log2(math.e)
LN2 = math.log(2.0)
SEND = jnp.bfloat16
ROWS = CAP * PER
PAIRS = ROWS // 2
BACK = PAIRS + 1
HALF = HEAD // 2
NT = (((1,), (1,)), ((), ()))
VMEM = pl.BlockSpec(memory_space=pltpu.VMEM)
SMEM = pl.BlockSpec(memory_space=pltpu.SMEM)
ANY = pl.BlockSpec(memory_space=pl.ANY)
in_smem = functools.partial(pltpu.with_memory_space_constraint, memory_space=pltpu.SMEM)
in_vmem = functools.partial(pltpu.with_memory_space_constraint, memory_space=pltpu.VMEM)


def slots_of(routes_ref, requests):
    routes = [routes_ref[r] for r in range(requests)]
    ranks = []
    for r in range(requests):
        rank = jnp.int32(0)
        for e in range(r):
            rank = rank + jnp.where(routes[e] == routes[r], 1, 0)
        ranks.append(rank)
    return routes, ranks


def pack_queries(groups, splits, routes_ref, q_ref, out_ref, rows_ref, x_ref):
    requests = q_ref.shape[0]
    routes, ranks = slots_of(routes_ref, requests)
    q = q_ref[...].astype(jnp.float32)
    for k in range(KVH):
        for h in range(PER):
            x_ref[h * requests:(h + 1) * requests, k * HEAD:(k + 1) * HEAD] = q[
                :, (k * PER + h) * HEAD:(k * PER + h + 1) * HEAD
            ]
    x = x_ref[...].astype(jnp.bfloat16)
    cols = PER * requests
    total = groups * ROWS
    row = lax.broadcasted_iota(jnp.int32, (total, cols), 0)
    col = lax.broadcasted_iota(jnp.int32, (total, cols), 1)
    wanted = jnp.full((total, cols), -1, jnp.int32)
    for r in range(requests):
        wanted = jnp.where(col % requests == r, routes[r] * CAP + ranks[r], wanted)
    pick = (row // PER == wanted) & (row % PER == col // requests)
    placed = jnp.dot(
        pick.astype(jnp.float32).astype(jnp.bfloat16), x, preferred_element_type=jnp.float32
    ).astype(jnp.bfloat16)
    for g in range(groups):
        for k in range(KVH):
            tile = placed[g * ROWS:(g + 1) * ROWS, k * HEAD:(k + 1) * HEAD]
            for t in range(splits):
                out_ref[g, t, k] = tile
    mine = requests * PER
    row = lax.broadcasted_iota(jnp.int32, (mine, cols), 0)
    col = lax.broadcasted_iota(jnp.int32, (mine, cols), 1)
    turn = (row // PER == col % requests) & (row % PER == col // requests)
    turned = jnp.dot(
        turn.astype(jnp.float32).astype(jnp.bfloat16), x, preferred_element_type=jnp.float32
    )
    for r in range(requests):
        for k in range(KVH):
            rows_ref[r, k * PER:(k + 1) * PER, :] = turned[
                r * PER:(r + 1) * PER, k * HEAD:(k + 1) * HEAD
            ]


def prepare(groups, splits, routes_in, q_in, kv_ref, out_ref, rows_ref, routes_ref, *refs):
    blocks, (q_ref, x_ref, sems) = refs[:KVH], refs[KVH:]
    mine = lax.axis_index("seq") % KVH
    first = [
        pltpu.make_async_copy(routes_in, routes_ref, sems.at[KVH]),
        pltpu.make_async_copy(q_in, q_ref, sems.at[KVH + 1]),
    ]
    later = []
    for j in range(KVH):
        start = pl.multiple_of(jnp.bitwise_xor(mine, j) * HEAD, HEAD)
        later.append(
            pltpu.make_async_copy(kv_ref.at[0, :, :, pl.ds(start, HEAD)], blocks[j], sems.at[j])
        )
    for copy in first + later:
        copy.start()
    for copy in first:
        copy.wait()
    pack_queries(groups, splits, routes_ref, q_ref, out_ref, rows_ref, x_ref)
    for copy in later:
        copy.wait()


def suffix_kernel(len_in, rows_ref, new_in, kv_in, out_ref, stat_ref, len_ref, new_ref, kv_ref, sems):
    requests = rows_ref.shape[0]
    small = [
        pltpu.make_async_copy(len_in, len_ref, sems.at[2 * requests]),
        pltpu.make_async_copy(new_in, new_ref, sems.at[2 * requests + 1]),
    ]
    cached = [
        [
            pltpu.make_async_copy(kv_in.at[r, j], kv_ref.at[r, j], sems.at[2 * r + j])
            for r in range(requests)
        ]
        for j in range(2)
    ]
    for copy in small + cached[0] + cached[1]:
        copy.start()
    zero = jnp.zeros((PER, HEAD), jnp.float32)
    lane = lax.broadcasted_iota(jnp.int32, (HEADS, HEAD), 1)
    for copy in small:
        copy.wait()
    news, owns, raws = [], [], []
    for r in range(requests):
        q = rows_ref[r]
        wide = jnp.concatenate(
            [
                jnp.concatenate(
                    [q[k * PER:(k + 1) * PER] if j == k else zero for j in range(KVH)], axis=1
                )
                for k in range(KVH)
            ],
            axis=0,
        ).astype(jnp.bfloat16)
        new = new_ref[r].astype(jnp.float32)
        news.append(new)
        owns.append(
            jnp.concatenate(
                [
                    jnp.sum(
                        q[k * PER:(k + 1) * PER] * new[0:1, k * HEAD:(k + 1) * HEAD],
                        axis=1,
                        keepdims=True,
                    )
                    for k in range(KVH)
                ],
                axis=0,
            )
        )
        cached[0][r].wait()
        raw = lax.dot_general(wide, kv_ref[r, 0], NT, preferred_element_type=jnp.float32)
        live = lax.broadcasted_iota(jnp.int32, raw.shape, 1) < len_ref[r]
        raws.append(jnp.where(live, raw, -jnp.inf))
    weights, own_weights = [], []
    for r in range(requests):
        top = jnp.maximum(jnp.max(raws[r], axis=1, keepdims=True), owns[r])
        weight = jnp.exp2((raws[r] - top) * (SCALE * LOG2E))
        own_weight = jnp.exp2((owns[r] - top) * (SCALE * LOG2E))
        total = jnp.sum(weight, axis=1, keepdims=True) + own_weight
        stat_ref[r] = jnp.where(lane == 0, top * SCALE, total)
        weights.append(weight.astype(jnp.bfloat16))
        own_weights.append(own_weight.astype(jnp.bfloat16).astype(jnp.float32))
    for r in range(requests):
        cached[1][r].wait()
        full = jnp.dot(weights[r], kv_ref[r, 1], preferred_element_type=jnp.float32)
        for k in range(KVH):
            rows = slice(k * PER, (k + 1) * PER)
            cols = slice(k * HEAD, (k + 1) * HEAD)
            out_ref[r, rows, :] = full[rows, cols] + own_weights[r][rows] * news[r][1:2, cols]


def prefix_kernel(q_ref, *refs):
    parts, out_ref = refs[:-1], refs[-1]
    keys = jnp.concatenate([part[0] for part in parts], axis=0)
    values = jnp.concatenate([part[1] for part in parts], axis=0)
    sources = q_ref.shape[0]
    step = HEAD // ROWS
    shape = (step * ROWS, HEAD)
    diagonal = lax.broadcasted_iota(jnp.int32, shape, 0) == lax.broadcasted_iota(jnp.int32, shape, 1)
    low = lax.broadcasted_iota(jnp.int32, (1, HEAD), 1) < HALF

    def block(i):
        q = q_ref[pl.ds(i * step, step)].reshape(shape)
        raw = lax.dot_general(q, keys, NT, preferred_element_type=jnp.float32)
        top = jnp.max(raw, axis=1, keepdims=True)
        weight = jnp.exp2((raw - top) * (SCALE * LOG2E))
        total = jnp.sum(weight, axis=1, keepdims=True)
        out = jnp.dot(weight.astype(jnp.bfloat16), values, preferred_element_type=jnp.float32)
        out = (out / total).astype(SEND)
        level = top * SCALE + jnp.log(total)
        level = jnp.sum(jnp.where(diagonal, level, 0.0), axis=0, keepdims=True)
        first = level.astype(SEND).astype(jnp.float32)
        rest = level - first
        second = rest.astype(SEND).astype(jnp.float32)
        third = rest - second
        turned = [pltpu.roll(piece, HALF, 1) for piece in (first, second, third)]
        halves = [
            jnp.concatenate([jnp.where(low, first, turned[1]), third], axis=0).astype(SEND),
            jnp.concatenate([jnp.where(low, turned[0], second), turned[2]], axis=0).astype(SEND),
        ]
        for s in range(step):
            at = (i * step + s) * BACK
            out_ref[pl.ds(at, PAIRS)] = out[s * ROWS:(s + 1) * ROWS].reshape(PAIRS, 2, HEAD)
            out_ref[at + PAIRS] = halves[s // (step // 2)]

    if sources // step <= 4:
        for i in range(sources // step):
            block(i)
    else:
        lax.fori_loop(0, sources // step, lambda i, c: (block(i), c)[1], 0)


def join_kernel(splits, routes_ref, back_ref, suffix_ref, stat_ref, out_ref):
    requests = out_ref.shape[0]
    routes, ranks = slots_of(routes_ref, requests)
    step = HEAD // ROWS // 2
    place = lax.axis_index("seq") % step * ROWS
    lane = lax.broadcasted_iota(jnp.int32, (PER, HEAD), 1)
    head = lax.broadcasted_iota(jnp.int32, (PER, HEAD), 0)
    pieces = [[None] * requests for _ in range(KVH)]
    for r in range(requests):
        stats = stat_ref[r]
        once = lane == head + (place + ranks[r] * PER)
        twice = lane % HALF == head + (place + ranks[r] * PER)
        for k in range(KVH):
            rows = slice(k * PER, (k + 1) * PER)
            levels, parts = [], []
            for t in range(splits):
                at = ((routes[r] * splits + t) * KVH + k) * BACK
                pair = back_ref[pl.ds(at + ranks[r] * (PER // 2), PER // 2)]
                parts.append(pair.reshape(PER, HEAD).astype(jnp.float32))
                stat = back_ref[at + PAIRS].astype(jnp.float32)
                stat = jnp.where(twice, stat[0:1], 0.0) + jnp.where(once, stat[1:2], 0.0)
                levels.append(jnp.sum(stat, axis=1, keepdims=True))
            suffix_top = stats[rows, 0:1]
            top = suffix_top
            for level in levels:
                top = jnp.maximum(top, level)
            from_suffix = jnp.exp(suffix_top - top)
            numer = from_suffix * suffix_ref[r, rows, :]
            denom = from_suffix * stats[rows, 1:2]
            for level, part in zip(levels, parts):
                from_prefix = jnp.exp(level - top)
                numer = numer + from_prefix * part
                denom = denom + from_prefix
            pieces[k][r] = numer / denom
    stacked = jnp.concatenate(
        [jnp.concatenate(pieces[k], axis=0) for k in range(KVH)], axis=1
    ).astype(jnp.bfloat16)
    mine = requests * PER
    row = lax.broadcasted_iota(jnp.int32, (PER * 8, mine), 0)
    col = lax.broadcasted_iota(jnp.int32, (PER * 8, mine), 1)
    turn = (row % 8 == col // PER) & (row // 8 == col % PER)
    turned = jnp.dot(
        turn.astype(jnp.float32).astype(jnp.bfloat16), stacked, preferred_element_type=jnp.float32
    ).astype(jnp.bfloat16)
    turned = turned.astype(jnp.float32)
    for k in range(KVH):
        for h in range(PER):
            out_ref[:, (k * PER + h) * HEAD:(k * PER + h + 1) * HEAD] = turned[
                h * 8:h * 8 + requests, k * HEAD:(k + 1) * HEAD
            ].astype(jnp.bfloat16)


def on_device(queries, new_kv, suffix_kv, suffix_len, prefix_of, prefix_kv):
    groups = lax.axis_size("grp")
    seq = lax.axis_size("seq")
    splits = seq // KVH
    requests = queries.shape[0]
    span = suffix_kv.shape[2]
    here = prefix_kv.shape[2]
    everyone = ("grp", "seq")
    routes = prefix_of.reshape(requests)

    outgoing, rows, routes, *blocks = pl.pallas_call(
        functools.partial(prepare, groups, splits),
        out_shape=[
            jax.ShapeDtypeStruct((groups, splits, KVH, ROWS, HEAD), jnp.bfloat16),
            pltpu.VMEM((requests, HEADS, HEAD), jnp.float32),
            pltpu.SMEM((requests,), jnp.int32),
        ]
        + [pltpu.VMEM((2, here, HEAD), jnp.bfloat16)] * KVH,
        in_specs=[ANY, ANY, ANY],
        out_specs=[VMEM, VMEM, SMEM] + [VMEM] * KVH,
        scratch_shapes=[
            pltpu.VMEM((requests, HEADS * HEAD), jnp.bfloat16),
            pltpu.VMEM((PER * requests, KVH * HEAD), jnp.float32),
            pltpu.SemaphoreType.DMA((KVH + 2,)),
        ],
        name="prepare",
    )(routes, queries, prefix_kv)
    parts = [blocks[0]]
    for j in reversed(range(1, KVH)):
        parts.append(lax.ppermute(blocks[j], "seq", [(s, s ^ j) for s in range(seq)]))

    arrived = lax.all_to_all(
        outgoing.reshape(groups * seq, ROWS, HEAD), everyone, split_axis=0, concat_axis=0, tiled=True
    )

    suffix_out, suffix_stat = pl.pallas_call(
        suffix_kernel,
        out_shape=(
            pltpu.VMEM((requests, HEADS, HEAD), jnp.float32),
            pltpu.VMEM((requests, HEADS, HEAD), jnp.float32),
        ),
        in_specs=[ANY, VMEM, ANY, ANY],
        out_specs=(VMEM, VMEM),
        scratch_shapes=[
            pltpu.SMEM((requests,), jnp.int32),
            pltpu.VMEM(new_kv.shape, jnp.bfloat16),
            pltpu.VMEM(suffix_kv.shape, jnp.bfloat16),
            pltpu.SemaphoreType.DMA((2 * requests + 2,)),
        ],
        cost_estimate=pl.CostEstimate(
            flops=4 * requests * HEADS * KVH * HEAD * span,
            bytes_accessed=2 * suffix_kv.size,
            transcendentals=requests * HEADS * span,
        ),
        name="suffix_attention",
    )(suffix_len, in_vmem(rows), new_kv, suffix_kv)

    arrived, suffix_out, suffix_stat = lax.optimization_barrier(
        (arrived, suffix_out, suffix_stat)
    )

    back = pl.pallas_call(
        prefix_kernel,
        out_shape=pltpu.VMEM((groups * seq * BACK, 2, HEAD), SEND),
        in_specs=[VMEM] * (1 + KVH),
        out_specs=VMEM,
        compiler_params=pltpu.CompilerParams(vmem_limit_bytes=32 * 1024 * 1024),
        name="prefix_attention",
    )(arrived, *parts)

    home = in_vmem(lax.all_to_all(back, everyone, split_axis=0, concat_axis=0, tiled=True))

    return pl.pallas_call(
        functools.partial(join_kernel, splits),
        out_shape=jax.ShapeDtypeStruct((requests, HEADS * HEAD), jnp.bfloat16),
        in_specs=[SMEM, VMEM, VMEM, VMEM],
        out_specs=VMEM,
        name="join",
    )(in_smem(routes), home, in_vmem(suffix_out), in_vmem(suffix_stat))


def solution(mesh):
    in_specs = (
        P(("grp", "seq"), None),
        P(("grp", "seq"), None, None),
        P(("grp", "seq"), None, None, None),
        P(("grp", "seq")),
        P(("grp", "seq"), None),
        P("grp", None, "seq", None),
    )
    out_specs = P(("grp", "seq"), None)
    return jax.shard_map(
        on_device, mesh=mesh, in_specs=in_specs, out_specs=out_specs, check_vma=False
    )
```

```python
import functools
import math

import jax
import jax.numpy as jnp
from jax import lax
from jax.experimental import pallas as pl
from jax.experimental.pallas import tpu as pltpu
from jax.sharding import PartitionSpec as P

HEADS = 64
KVH = 8
HEAD = 128
CAP = 2
PER = HEADS // KVH
SCALE = HEAD ** (-0.5)
LOG2E = math.log2(math.e)
LN2 = math.log(2.0)
SEND = jnp.bfloat16
ROWS = CAP * PER
PAIRS = ROWS // 2
BACK = PAIRS + 1
HALF = HEAD // 2
NT = (((1,), (1,)), ((), ()))
VMEM = pl.BlockSpec(memory_space=pltpu.VMEM)
SMEM = pl.BlockSpec(memory_space=pltpu.SMEM)
ANY = pl.BlockSpec(memory_space=pl.ANY)
in_smem = functools.partial(pltpu.with_memory_space_constraint, memory_space=pltpu.SMEM)
in_vmem = functools.partial(pltpu.with_memory_space_constraint, memory_space=pltpu.VMEM)


def slots_of(routes_ref, requests):
    routes = [routes_ref[r] for r in range(requests)]
    ranks = []
    for r in range(requests):
        rank = jnp.int32(0)
        for e in range(r):
            rank = rank + jnp.where(routes[e] == routes[r], 1, 0)
        ranks.append(rank)
    return routes, ranks


def pack_queries(groups, splits, routes_ref, q_ref, out_ref, rows_ref, x_ref):
    requests = q_ref.shape[0]
    routes, ranks = slots_of(routes_ref, requests)
    q = q_ref[...].astype(jnp.float32)
    for k in range(KVH):
        for h in range(PER):
            x_ref[h * requests:(h + 1) * requests, k * HEAD:(k + 1) * HEAD] = q[
                :, (k * PER + h) * HEAD:(k * PER + h + 1) * HEAD
            ]
    x = x_ref[...].astype(jnp.bfloat16)
    cols = PER * requests
    total = groups * ROWS
    row = lax.broadcasted_iota(jnp.int32, (total, cols), 0)
    col = lax.broadcasted_iota(jnp.int32, (total, cols), 1)
    wanted = jnp.full((total, cols), -1, jnp.int32)
    for r in range(requests):
        wanted = jnp.where(col % requests == r, routes[r] * CAP + ranks[r], wanted)
    pick = (row // PER == wanted) & (row % PER == col // requests)
    placed = jnp.dot(
        pick.astype(jnp.float32).astype(jnp.bfloat16), x, preferred_element_type=jnp.float32
    ).astype(jnp.bfloat16)
    for g in range(groups):
        for k in range(KVH):
            tile = placed[g * ROWS:(g + 1) * ROWS, k * HEAD:(k + 1) * HEAD]
            for t in range(splits):
                out_ref[(g * splits + t) * KVH + k] = tile
    mine = requests * PER
    row = lax.broadcasted_iota(jnp.int32, (mine, cols), 0)
    col = lax.broadcasted_iota(jnp.int32, (mine, cols), 1)
    turn = (row // PER == col % requests) & (row % PER == col // requests)
    turned = jnp.dot(
        turn.astype(jnp.float32).astype(jnp.bfloat16), x, preferred_element_type=jnp.float32
    )
    for r in range(requests):
        for k in range(KVH):
            rows_ref[r, k * PER:(k + 1) * PER, :] = turned[
                r * PER:(r + 1) * PER, k * HEAD:(k + 1) * HEAD
            ]


def prepare(groups, splits, routes_in, q_in, kv_ref, out_ref, rows_ref, routes_ref, *refs):
    blocks, (q_ref, x_ref, sems) = refs[:KVH], refs[KVH:]
    mine = lax.axis_index("seq") % KVH
    first = [
        pltpu.make_async_copy(routes_in, routes_ref, sems.at[KVH]),
        pltpu.make_async_copy(q_in, q_ref, sems.at[KVH + 1]),
    ]
    later = []
    for j in range(KVH):
        start = pl.multiple_of(jnp.bitwise_xor(mine, j) * HEAD, HEAD)
        later.append(
            pltpu.make_async_copy(kv_ref.at[0, :, :, pl.ds(start, HEAD)], blocks[j], sems.at[j])
        )
    for copy in first + later:
        copy.start()
    for copy in first:
        copy.wait()
    pack_queries(groups, splits, routes_ref, q_ref, out_ref, rows_ref, x_ref)
    for copy in later:
        copy.wait()


def suffix_kernel(len_in, rows_ref, new_in, kv_in, out_ref, stat_ref, len_ref, new_ref, kv_ref, sems):
    requests = rows_ref.shape[0]
    small = [
        pltpu.make_async_copy(len_in, len_ref, sems.at[2 * requests]),
        pltpu.make_async_copy(new_in, new_ref, sems.at[2 * requests + 1]),
    ]
    cached = [
        [
            pltpu.make_async_copy(kv_in.at[r, j], kv_ref.at[r, j], sems.at[2 * r + j])
            for r in range(requests)
        ]
        for j in range(2)
    ]
    for copy in small + cached[0] + cached[1]:
        copy.start()
    lane = lax.broadcasted_iota(jnp.int32, (HEADS, HEAD), 1)
    upper = lax.broadcasted_iota(jnp.int32, (2 * PER, HEAD), 0) < PER
    wides = []
    for r in range(requests):
        q = rows_ref[r]
        wides.append([])
        for pair in range(KVH // 2):
            two = q[2 * pair * PER:2 * (pair + 1) * PER]
            wides[r].append(
                jnp.concatenate(
                    [jnp.where(upper, two, 0.0), jnp.where(upper, 0.0, two)], axis=1
                ).astype(jnp.bfloat16)
            )
    for copy in small:
        copy.wait()
    news, owns, raws = [], [], []
    for r in range(requests):
        q = rows_ref[r]
        new = new_ref[r].astype(jnp.float32)
        news.append(new)
        owns.append(
            jnp.concatenate(
                [
                    jnp.sum(
                        q[k * PER:(k + 1) * PER] * new[0:1, k * HEAD:(k + 1) * HEAD],
                        axis=1,
                        keepdims=True,
                    )
                    for k in range(KVH)
                ],
                axis=0,
            )
        )
    for r in range(requests):
        cached[0][r].wait()
        raw = jnp.concatenate(
            [
                lax.dot_general(
                    wides[r][pair],
                    kv_ref[r, 0, :, 2 * pair * HEAD:2 * (pair + 1) * HEAD],
                    NT,
                    preferred_element_type=jnp.float32,
                )
                for pair in range(KVH // 2)
            ],
            axis=0,
        )
        live = lax.broadcasted_iota(jnp.int32, raw.shape, 1) < len_ref[r]
        raws.append(jnp.where(live, raw, -jnp.inf))
    weights, own_weights = [], []
    for r in range(requests):
        top = jnp.maximum(jnp.max(raws[r], axis=1, keepdims=True), owns[r])
        weight = jnp.exp2((raws[r] - top) * (SCALE * LOG2E))
        own_weight = jnp.exp2((owns[r] - top) * (SCALE * LOG2E))
        total = jnp.sum(weight, axis=1, keepdims=True) + own_weight
        stat_ref[r] = jnp.where(lane == 0, top * SCALE, total)
        weights.append(weight.astype(jnp.bfloat16))
        own_weights.append(own_weight.astype(jnp.bfloat16).astype(jnp.float32))
    for r in range(requests):
        cached[1][r].wait()
        for pair in range(KVH // 2):
            both = jnp.dot(
                weights[r][2 * pair * PER:2 * (pair + 1) * PER],
                kv_ref[r, 1, :, 2 * pair * HEAD:2 * (pair + 1) * HEAD],
                preferred_element_type=jnp.float32,
            )
            for j in range(2):
                k = 2 * pair + j
                rows = slice(k * PER, (k + 1) * PER)
                cols = slice(k * HEAD, (k + 1) * HEAD)
                out_ref[r, rows, :] = (
                    both[j * PER:(j + 1) * PER, j * HEAD:(j + 1) * HEAD]
                    + own_weights[r][rows] * news[r][1:2, cols]
                )


def prefix_kernel(q_ref, *refs):
    parts, out_ref = refs[:-1], refs[-1]
    keys = jnp.concatenate([part[0] for part in parts], axis=0)
    values = jnp.concatenate([part[1] for part in parts], axis=0)
    sources = q_ref.shape[0]
    step = HEAD // ROWS
    shape = (step * ROWS, HEAD)
    diagonal = lax.broadcasted_iota(jnp.int32, shape, 0) == lax.broadcasted_iota(jnp.int32, shape, 1)
    low = lax.broadcasted_iota(jnp.int32, (1, HEAD), 1) < HALF

    def score(i):
        q = q_ref[pl.ds(i * step, step)].reshape(shape)
        return lax.dot_general(q, keys, NT, preferred_element_type=jnp.float32)

    def weigh(raw):
        top = jnp.max(raw, axis=1, keepdims=True)
        weight = jnp.exp2((raw - top) * (SCALE * LOG2E))
        total = jnp.sum(weight, axis=1, keepdims=True)
        return top, weight.astype(jnp.bfloat16), total

    def store(i, top, weight, total):
        out = jnp.dot(weight, values, preferred_element_type=jnp.float32)
        out = (out / total).astype(SEND)
        level = top * SCALE + jnp.log(total)
        level = jnp.sum(jnp.where(diagonal, level, 0.0), axis=0, keepdims=True)
        first = level.astype(SEND).astype(jnp.float32)
        rest = level - first
        second = rest.astype(SEND).astype(jnp.float32)
        third = rest - second
        turned = [pltpu.roll(piece, HALF, 1) for piece in (first, second, third)]
        halves = [
            jnp.concatenate([jnp.where(low, first, turned[1]), third], axis=0).astype(SEND),
            jnp.concatenate([jnp.where(low, turned[0], second), turned[2]], axis=0).astype(SEND),
        ]
        for s in range(step):
            at = (i * step + s) * BACK
            out_ref[pl.ds(at, PAIRS)] = out[s * ROWS:(s + 1) * ROWS].reshape(PAIRS, 2, HEAD)
            out_ref[at + PAIRS] = halves[s // (step // 2)]

    def several(start, count):
        ahead, done = score(start), None
        for i in range(count):
            raw = ahead
            if i + 1 < count:
                ahead = score(start + i + 1)
            ready = weigh(raw)
            if done is not None:
                store(start + i - 1, *done)
            done = ready
        store(start + count - 1, *done)

    blocks = sources // step
    count = 4 if blocks % 4 == 0 else 1
    if blocks == count:
        several(0, count)
    else:
        lax.fori_loop(0, blocks // count, lambda i, c: (several(i * count, count), c)[1], 0)


def join_kernel(splits, routes_ref, back_ref, suffix_ref, stat_ref, out_ref):
    requests = out_ref.shape[0]
    routes, ranks = slots_of(routes_ref, requests)
    step = HEAD // ROWS // 2
    place = lax.axis_index("seq") % step * ROWS
    lane = lax.broadcasted_iota(jnp.int32, (PER, HEAD), 1)
    head = lax.broadcasted_iota(jnp.int32, (PER, HEAD), 0)
    pieces = [[None] * requests for _ in range(KVH)]
    for r in range(requests):
        stats = stat_ref[r]
        once = lane == head + (place + ranks[r] * PER)
        twice = lane % HALF == head + (place + ranks[r] * PER)
        for k in range(KVH):
            rows = slice(k * PER, (k + 1) * PER)
            levels, parts = [], []
            for t in range(splits):
                at = ((routes[r] * splits + t) * KVH + k) * BACK
                pair = back_ref[pl.ds(at + ranks[r] * (PER // 2), PER // 2)]
                parts.append(pair.reshape(PER, HEAD).astype(jnp.float32))
                stat = back_ref[at + PAIRS].astype(jnp.float32)
                stat = jnp.where(twice, stat[0:1], 0.0) + jnp.where(once, stat[1:2], 0.0)
                levels.append(jnp.sum(stat, axis=1, keepdims=True))
            suffix_top = stats[rows, 0:1]
            top = suffix_top
            for level in levels:
                top = jnp.maximum(top, level)
            from_suffix = jnp.exp(suffix_top - top)
            numer = from_suffix * suffix_ref[r, rows, :]
            denom = from_suffix * stats[rows, 1:2]
            for level, part in zip(levels, parts):
                from_prefix = jnp.exp(level - top)
                numer = numer + from_prefix * part
                denom = denom + from_prefix
            pieces[k][r] = numer / denom
    stacked = jnp.concatenate(
        [jnp.concatenate(pieces[k], axis=0) for k in range(KVH)], axis=1
    ).astype(jnp.bfloat16)
    mine = requests * PER
    row = lax.broadcasted_iota(jnp.int32, (PER * 8, mine), 0)
    col = lax.broadcasted_iota(jnp.int32, (PER * 8, mine), 1)
    turn = (row % 8 == col // PER) & (row // 8 == col % PER)
    turned = jnp.dot(
        turn.astype(jnp.float32).astype(jnp.bfloat16), stacked, preferred_element_type=jnp.float32
    ).astype(jnp.bfloat16)
    turned = turned.astype(jnp.float32)
    for k in range(KVH):
        for h in range(PER):
            out_ref[:, (k * PER + h) * HEAD:(k * PER + h + 1) * HEAD] = turned[
                h * 8:h * 8 + requests, k * HEAD:(k + 1) * HEAD
            ].astype(jnp.bfloat16)


def on_device(queries, new_kv, suffix_kv, suffix_len, prefix_of, prefix_kv):
    groups = lax.axis_size("grp")
    seq = lax.axis_size("seq")
    splits = seq // KVH
    requests = queries.shape[0]
    span = suffix_kv.shape[2]
    here = prefix_kv.shape[2]
    everyone = ("grp", "seq")
    routes = prefix_of.reshape(requests)

    outgoing, rows, routes, *blocks = pl.pallas_call(
        functools.partial(prepare, groups, splits),
        out_shape=[
            pltpu.VMEM((groups * seq, ROWS, HEAD), jnp.bfloat16),
            pltpu.VMEM((requests, HEADS, HEAD), jnp.float32),
            pltpu.SMEM((requests,), jnp.int32),
        ]
        + [pltpu.VMEM((2, here, HEAD), jnp.bfloat16)] * KVH,
        in_specs=[ANY, ANY, ANY],
        out_specs=[VMEM, VMEM, SMEM] + [VMEM] * KVH,
        scratch_shapes=[
            pltpu.VMEM((requests, HEADS * HEAD), jnp.bfloat16),
            pltpu.VMEM((PER * requests, KVH * HEAD), jnp.float32),
            pltpu.SemaphoreType.DMA((KVH + 2,)),
        ],
        name="prepare",
    )(routes, queries, prefix_kv)
    parts = [blocks[0]]
    for j in reversed(range(1, KVH)):
        parts.append(lax.ppermute(blocks[j], "seq", [(s, s ^ j) for s in range(seq)]))

    arrived = lax.all_to_all(
        in_vmem(outgoing), everyone, split_axis=0, concat_axis=0, tiled=True
    )

    suffix_out, suffix_stat = pl.pallas_call(
        suffix_kernel,
        out_shape=(
            pltpu.VMEM((requests, HEADS, HEAD), jnp.float32),
            pltpu.VMEM((requests, HEADS, HEAD), jnp.float32),
        ),
        in_specs=[ANY, VMEM, ANY, ANY],
        out_specs=(VMEM, VMEM),
        scratch_shapes=[
            pltpu.SMEM((requests,), jnp.int32),
            pltpu.VMEM(new_kv.shape, jnp.bfloat16),
            pltpu.VMEM(suffix_kv.shape, jnp.bfloat16),
            pltpu.SemaphoreType.DMA((2 * requests + 2,)),
        ],
        cost_estimate=pl.CostEstimate(
            flops=4 * requests * HEADS * KVH * HEAD * span,
            bytes_accessed=2 * suffix_kv.size,
            transcendentals=requests * HEADS * span,
        ),
        name="suffix_attention",
    )(suffix_len, in_vmem(rows), new_kv, suffix_kv)

    arrived, suffix_out, suffix_stat = lax.optimization_barrier(
        (arrived, suffix_out, suffix_stat)
    )

    back = pl.pallas_call(
        prefix_kernel,
        out_shape=pltpu.VMEM((groups * seq * BACK, 2, HEAD), SEND),
        in_specs=[VMEM] * (1 + KVH),
        out_specs=VMEM,
        compiler_params=pltpu.CompilerParams(vmem_limit_bytes=32 * 1024 * 1024),
        name="prefix_attention",
    )(arrived, *parts)

    home = in_vmem(lax.all_to_all(back, everyone, split_axis=0, concat_axis=0, tiled=True))

    return pl.pallas_call(
        functools.partial(join_kernel, splits),
        out_shape=jax.ShapeDtypeStruct((requests, HEADS * HEAD), jnp.bfloat16),
        in_specs=[SMEM, VMEM, VMEM, VMEM],
        out_specs=VMEM,
        name="join",
    )(in_smem(routes), home, in_vmem(suffix_out), in_vmem(suffix_stat))


def solution(mesh):
    in_specs = (
        P(("grp", "seq"), None),
        P(("grp", "seq"), None, None),
        P(("grp", "seq"), None, None, None),
        P(("grp", "seq")),
        P(("grp", "seq"), None),
        P("grp", None, "seq", None),
    )
    out_specs = P(("grp", "seq"), None)
    return jax.shard_map(
        on_device, mesh=mesh, in_specs=in_specs, out_specs=out_specs, check_vma=False
    )
```

```python
import functools
import math

import jax
import jax.numpy as jnp
from jax import lax
from jax.experimental import pallas as pl
from jax.experimental.pallas import tpu as pltpu
from jax.sharding import PartitionSpec as P

HEADS = 64
KVH = 8
HEAD = 128
CAP = 2
PER = HEADS // KVH
SCALE = HEAD ** (-0.5)
LOG2E = math.log2(math.e)
LN2 = math.log(2.0)
SEND = jnp.bfloat16
ROWS = CAP * PER
PAIRS = ROWS // 2
BACK = PAIRS + 1
HALF = HEAD // 2
NT = (((1,), (1,)), ((), ()))
VMEM = pl.BlockSpec(memory_space=pltpu.VMEM)
SMEM = pl.BlockSpec(memory_space=pltpu.SMEM)
ANY = pl.BlockSpec(memory_space=pl.ANY)
in_smem = functools.partial(pltpu.with_memory_space_constraint, memory_space=pltpu.SMEM)
in_vmem = functools.partial(pltpu.with_memory_space_constraint, memory_space=pltpu.VMEM)


def slots_of(routes_ref, requests):
    routes = [routes_ref[r] for r in range(requests)]
    ranks = []
    for r in range(requests):
        rank = jnp.int32(0)
        for e in range(r):
            rank = rank + jnp.where(routes[e] == routes[r], 1, 0)
        ranks.append(rank)
    return routes, ranks


def pack_queries(groups, splits, routes_ref, q_ref, out_ref, rows_ref, x_ref):
    requests = q_ref.shape[0]
    routes, ranks = slots_of(routes_ref, requests)
    q = q_ref[...].astype(jnp.float32)
    for k in range(KVH):
        for h in range(PER):
            x_ref[h * requests:(h + 1) * requests, k * HEAD:(k + 1) * HEAD] = q[
                :, (k * PER + h) * HEAD:(k * PER + h + 1) * HEAD
            ]
    x = x_ref[...].astype(jnp.bfloat16)
    cols = PER * requests
    total = groups * ROWS
    row = lax.broadcasted_iota(jnp.int32, (total, cols), 0)
    col = lax.broadcasted_iota(jnp.int32, (total, cols), 1)
    wanted = jnp.full((total, cols), -1, jnp.int32)
    for r in range(requests):
        wanted = jnp.where(col % requests == r, routes[r] * CAP + ranks[r], wanted)
    pick = (row // PER == wanted) & (row % PER == col // requests)
    placed = jnp.dot(
        pick.astype(jnp.float32).astype(jnp.bfloat16), x, preferred_element_type=jnp.float32
    ).astype(jnp.bfloat16)
    for g in range(groups):
        for k in range(KVH):
            tile = placed[g * ROWS:(g + 1) * ROWS, k * HEAD:(k + 1) * HEAD]
            for t in range(splits):
                out_ref[(g * splits + t) * KVH + k] = tile
    mine = requests * PER
    row = lax.broadcasted_iota(jnp.int32, (mine, cols), 0)
    col = lax.broadcasted_iota(jnp.int32, (mine, cols), 1)
    turn = (row // PER == col % requests) & (row % PER == col // requests)
    turned = jnp.dot(
        turn.astype(jnp.float32).astype(jnp.bfloat16), x, preferred_element_type=jnp.float32
    )
    for r in range(requests):
        for k in range(KVH):
            rows_ref[r, k * PER:(k + 1) * PER, :] = turned[
                r * PER:(r + 1) * PER, k * HEAD:(k + 1) * HEAD
            ]


def prepare(groups, splits, routes_in, q_in, kv_ref, out_ref, rows_ref, routes_ref, *refs):
    blocks, (q_ref, x_ref, sems) = refs[:5], refs[5:]
    mine = lax.axis_index("seq") % KVH
    first = [
        pltpu.make_async_copy(routes_in, routes_ref, sems.at[KVH]),
        pltpu.make_async_copy(q_in, q_ref, sems.at[KVH + 1]),
    ]
    later = []
    for j in range(KVH):
        start = pl.multiple_of(jnp.bitwise_xor(mine, j) * HEAD, HEAD)
        later.append(
            pltpu.make_async_copy(
                kv_ref.at[0, :, :, pl.ds(start, HEAD)],
                blocks[j] if j < 2 else blocks[1 + j // 2].at[j % 2],
                sems.at[j],
            )
        )
    for copy in first + later:
        copy.start()
    for copy in first:
        copy.wait()
    pack_queries(groups, splits, routes_ref, q_ref, out_ref, rows_ref, x_ref)
    for copy in later:
        copy.wait()


def suffix_kernel(len_in, rows_ref, new_in, kv_in, out_ref, stat_ref, len_ref, new_ref, kv_ref, sems):
    requests = rows_ref.shape[0]
    small = [
        pltpu.make_async_copy(len_in, len_ref, sems.at[2 * requests]),
        pltpu.make_async_copy(new_in, new_ref, sems.at[2 * requests + 1]),
    ]
    cached = [
        [
            pltpu.make_async_copy(kv_in.at[r, j], kv_ref.at[r, j], sems.at[2 * r + j])
            for r in range(requests)
        ]
        for j in range(2)
    ]
    for copy in small + cached[0] + cached[1]:
        copy.start()
    lane = lax.broadcasted_iota(jnp.int32, (HEADS, HEAD), 1)
    upper = lax.broadcasted_iota(jnp.int32, (2 * PER, HEAD), 0) < PER
    wides = []
    for r in range(requests):
        q = rows_ref[r]
        wides.append([])
        for pair in range(KVH // 2):
            two = q[2 * pair * PER:2 * (pair + 1) * PER]
            wides[r].append(
                jnp.concatenate(
                    [jnp.where(upper, two, 0.0), jnp.where(upper, 0.0, two)], axis=1
                ).astype(jnp.bfloat16)
            )
    for copy in small:
        copy.wait()
    news, owns, raws = [], [], []
    for r in range(requests):
        q = rows_ref[r]
        new = new_ref[r].astype(jnp.float32)
        news.append(new)
        owns.append(
            jnp.concatenate(
                [
                    jnp.sum(
                        q[k * PER:(k + 1) * PER] * new[0:1, k * HEAD:(k + 1) * HEAD],
                        axis=1,
                        keepdims=True,
                    )
                    for k in range(KVH)
                ],
                axis=0,
            )
        )
    for r in range(requests):
        cached[0][r].wait()
        raw = jnp.concatenate(
            [
                lax.dot_general(
                    wides[r][pair],
                    kv_ref[r, 0, :, 2 * pair * HEAD:2 * (pair + 1) * HEAD],
                    NT,
                    preferred_element_type=jnp.float32,
                )
                for pair in range(KVH // 2)
            ],
            axis=0,
        )
        live = lax.broadcasted_iota(jnp.int32, raw.shape, 1) < len_ref[r]
        raws.append(jnp.where(live, raw, -jnp.inf))
    weights, own_weights = [], []
    for r in range(requests):
        top = jnp.maximum(jnp.max(raws[r], axis=1, keepdims=True), owns[r])
        weight = jnp.exp2((raws[r] - top) * (SCALE * LOG2E))
        own_weight = jnp.exp2((owns[r] - top) * (SCALE * LOG2E))
        total = jnp.sum(weight, axis=1, keepdims=True) + own_weight
        stat_ref[r] = jnp.where(lane == 0, top * SCALE, total)
        weights.append(weight.astype(jnp.bfloat16))
        own_weights.append(own_weight.astype(jnp.bfloat16).astype(jnp.float32))
    for r in range(requests):
        cached[1][r].wait()
        for pair in range(KVH // 2):
            both = jnp.dot(
                weights[r][2 * pair * PER:2 * (pair + 1) * PER],
                kv_ref[r, 1, :, 2 * pair * HEAD:2 * (pair + 1) * HEAD],
                preferred_element_type=jnp.float32,
            )
            for j in range(2):
                k = 2 * pair + j
                rows = slice(k * PER, (k + 1) * PER)
                cols = slice(k * HEAD, (k + 1) * HEAD)
                out_ref[r, rows, :] = (
                    both[j * PER:(j + 1) * PER, j * HEAD:(j + 1) * HEAD]
                    + own_weights[r][rows] * news[r][1:2, cols]
                )


def prefix_kernel(q_ref, *refs):
    parts, out_ref = refs[:-1], refs[-1]
    views = [part for part in parts[:2]]
    views += [part.at[0] for part in parts[2:5]] + [part.at[1] for part in parts[5:]]
    keys = jnp.concatenate([view[0] for view in views], axis=0)
    values = jnp.concatenate([view[1] for view in views], axis=0)
    sources = q_ref.shape[0]
    step = HEAD // ROWS
    shape = (step * ROWS, HEAD)
    diagonal = lax.broadcasted_iota(jnp.int32, shape, 0) == lax.broadcasted_iota(jnp.int32, shape, 1)
    low = lax.broadcasted_iota(jnp.int32, (1, HEAD), 1) < HALF

    def score(i):
        q = q_ref[pl.ds(i * step, step)].reshape(shape)
        return lax.dot_general(q, keys, NT, preferred_element_type=jnp.float32)

    def weigh(raw):
        top = jnp.max(raw, axis=1, keepdims=True)
        weight = jnp.exp2((raw - top) * (SCALE * LOG2E))
        total = jnp.sum(weight, axis=1, keepdims=True)
        return top, weight.astype(jnp.bfloat16), total

    def store(i, top, weight, total):
        out = jnp.dot(weight, values, preferred_element_type=jnp.float32)
        out = (out / total).astype(SEND)
        level = top * SCALE + jnp.log(total)
        level = jnp.sum(jnp.where(diagonal, level, 0.0), axis=0, keepdims=True)
        first = level.astype(SEND).astype(jnp.float32)
        rest = level - first
        second = rest.astype(SEND).astype(jnp.float32)
        third = rest - second
        turned = [pltpu.roll(piece, HALF, 1) for piece in (first, second, third)]
        halves = [
            jnp.concatenate([jnp.where(low, first, turned[1]), third], axis=0).astype(SEND),
            jnp.concatenate([jnp.where(low, turned[0], second), turned[2]], axis=0).astype(SEND),
        ]
        for s in range(step):
            at = (i * step + s) * BACK
            out_ref[pl.ds(at, PAIRS)] = out[s * ROWS:(s + 1) * ROWS].reshape(PAIRS, 2, HEAD)
            out_ref[at + PAIRS] = halves[s // (step // 2)]

    def several(start, count):
        ahead, done = score(start), None
        for i in range(count):
            raw = ahead
            if i + 1 < count:
                ahead = score(start + i + 1)
            ready = weigh(raw)
            if done is not None:
                store(start + i - 1, *done)
            done = ready
        store(start + count - 1, *done)

    blocks = sources // step
    count = 4 if blocks % 4 == 0 else 1
    if blocks == count:
        several(0, count)
    else:
        lax.fori_loop(0, blocks // count, lambda i, c: (several(i * count, count), c)[1], 0)


def join_kernel(splits, routes_ref, back_ref, suffix_ref, stat_ref, out_ref):
    requests = out_ref.shape[0]
    routes, ranks = slots_of(routes_ref, requests)
    step = HEAD // ROWS // 2
    place = lax.axis_index("seq") % step * ROWS
    lane = lax.broadcasted_iota(jnp.int32, (PER, HEAD), 1)
    head = lax.broadcasted_iota(jnp.int32, (PER, HEAD), 0)
    pieces = [[None] * requests for _ in range(KVH)]
    for r in range(requests):
        stats = stat_ref[r]
        once = lane == head + (place + ranks[r] * PER)
        twice = lane % HALF == head + (place + ranks[r] * PER)
        for k in range(KVH):
            rows = slice(k * PER, (k + 1) * PER)
            levels, parts = [], []
            for t in range(splits):
                at = ((routes[r] * splits + t) * KVH + k) * BACK
                pair = back_ref[pl.ds(at + ranks[r] * (PER // 2), PER // 2)]
                parts.append(pair.reshape(PER, HEAD).astype(jnp.float32))
                stat = back_ref[at + PAIRS].astype(jnp.float32)
                stat = jnp.where(twice, stat[0:1], 0.0) + jnp.where(once, stat[1:2], 0.0)
                levels.append(jnp.sum(stat, axis=1, keepdims=True))
            suffix_top = stats[rows, 0:1]
            top = suffix_top
            for level in levels:
                top = jnp.maximum(top, level)
            from_suffix = jnp.exp(suffix_top - top)
            numer = from_suffix * suffix_ref[r, rows, :]
            denom = from_suffix * stats[rows, 1:2]
            for level, part in zip(levels, parts):
                from_prefix = jnp.exp(level - top)
                numer = numer + from_prefix * part
                denom = denom + from_prefix
            pieces[k][r] = numer / denom
    stacked = jnp.concatenate(
        [jnp.concatenate(pieces[k], axis=0) for k in range(KVH)], axis=1
    ).astype(jnp.bfloat16)
    mine = requests * PER
    row = lax.broadcasted_iota(jnp.int32, (PER * 8, mine), 0)
    col = lax.broadcasted_iota(jnp.int32, (PER * 8, mine), 1)
    turn = (row % 8 == col // PER) & (row // 8 == col % PER)
    turned = jnp.dot(
        turn.astype(jnp.float32).astype(jnp.bfloat16), stacked, preferred_element_type=jnp.float32
    ).astype(jnp.bfloat16)
    turned = turned.astype(jnp.float32)
    for k in range(KVH):
        for h in range(PER):
            out_ref[:, (k * PER + h) * HEAD:(k * PER + h + 1) * HEAD] = turned[
                h * 8:h * 8 + requests, k * HEAD:(k + 1) * HEAD
            ].astype(jnp.bfloat16)


def on_device(queries, new_kv, suffix_kv, suffix_len, prefix_of, prefix_kv):
    groups = lax.axis_size("grp")
    seq = lax.axis_size("seq")
    splits = seq // KVH
    requests = queries.shape[0]
    span = suffix_kv.shape[2]
    here = prefix_kv.shape[2]
    everyone = ("grp", "seq")
    routes = prefix_of.reshape(requests)

    outgoing, rows, routes, *blocks = pl.pallas_call(
        functools.partial(prepare, groups, splits),
        out_shape=[
            pltpu.VMEM((groups * seq, ROWS, HEAD), jnp.bfloat16),
            pltpu.VMEM((requests, HEADS, HEAD), jnp.float32),
            pltpu.SMEM((requests,), jnp.int32),
        ]
        + [pltpu.VMEM((2, here, HEAD), jnp.bfloat16)] * 2
        + [pltpu.VMEM((2, 2, here, HEAD), jnp.bfloat16)] * 3,
        in_specs=[ANY, ANY, ANY],
        out_specs=[VMEM, VMEM, SMEM] + [VMEM] * 5,
        scratch_shapes=[
            pltpu.VMEM((requests, HEADS * HEAD), jnp.bfloat16),
            pltpu.VMEM((PER * requests, KVH * HEAD), jnp.float32),
            pltpu.SemaphoreType.DMA((KVH + 2,)),
        ],
        name="prepare",
    )(routes, queries, prefix_kv)
    def swap(block, j):
        return lax.ppermute(block, "seq", [(s, s ^ j) for s in range(seq)])

    parts = [blocks[0], swap(blocks[1], 1)]
    pairs = [swap(blocks[1 + j // 2], j) for j in (6, 4, 2)]
    parts += pairs + [swap(pair, 1) for pair in pairs]

    arrived = lax.all_to_all(
        in_vmem(outgoing), everyone, split_axis=0, concat_axis=0, tiled=True
    )

    suffix_out, suffix_stat = pl.pallas_call(
        suffix_kernel,
        out_shape=(
            pltpu.VMEM((requests, HEADS, HEAD), jnp.float32),
            pltpu.VMEM((requests, HEADS, HEAD), jnp.float32),
        ),
        in_specs=[ANY, VMEM, ANY, ANY],
        out_specs=(VMEM, VMEM),
        scratch_shapes=[
            pltpu.SMEM((requests,), jnp.int32),
            pltpu.VMEM(new_kv.shape, jnp.bfloat16),
            pltpu.VMEM(suffix_kv.shape, jnp.bfloat16),
            pltpu.SemaphoreType.DMA((2 * requests + 2,)),
        ],
        cost_estimate=pl.CostEstimate(
            flops=4 * requests * HEADS * KVH * HEAD * span,
            bytes_accessed=2 * suffix_kv.size,
            transcendentals=requests * HEADS * span,
        ),
        name="suffix_attention",
    )(suffix_len, in_vmem(rows), new_kv, suffix_kv)

    arrived, suffix_out, suffix_stat = lax.optimization_barrier(
        (arrived, suffix_out, suffix_stat)
    )

    back = pl.pallas_call(
        prefix_kernel,
        out_shape=pltpu.VMEM((groups * seq * BACK, 2, HEAD), SEND),
        in_specs=[VMEM] * (1 + KVH),
        out_specs=VMEM,
        compiler_params=pltpu.CompilerParams(vmem_limit_bytes=32 * 1024 * 1024),
        name="prefix_attention",
    )(arrived, *parts)

    home = in_vmem(lax.all_to_all(back, everyone, split_axis=0, concat_axis=0, tiled=True))

    return pl.pallas_call(
        functools.partial(join_kernel, splits),
        out_shape=jax.ShapeDtypeStruct((requests, HEADS * HEAD), jnp.bfloat16),
        in_specs=[SMEM, VMEM, VMEM, VMEM],
        out_specs=VMEM,
        name="join",
    )(in_smem(routes), home, in_vmem(suffix_out), in_vmem(suffix_stat))


def solution(mesh):
    in_specs = (
        P(("grp", "seq"), None),
        P(("grp", "seq"), None, None),
        P(("grp", "seq"), None, None, None),
        P(("grp", "seq")),
        P(("grp", "seq"), None),
        P("grp", None, "seq", None),
    )
    out_specs = P(("grp", "seq"), None)
    return jax.shard_map(
        on_device, mesh=mesh, in_specs=in_specs, out_specs=out_specs, check_vma=False
    )
```

```python
import functools
import math

import jax
import jax.numpy as jnp
from jax import lax
from jax.experimental import pallas as pl
from jax.experimental.pallas import tpu as pltpu
from jax.sharding import PartitionSpec as P

HEADS = 64
KVH = 8
HEAD = 128
CAP = 2
PER = HEADS // KVH
SCALE = HEAD ** (-0.5)
LOG2E = math.log2(math.e)
LN2 = math.log(2.0)
SEND = jnp.bfloat16
ROWS = CAP * PER
PAIRS = ROWS // 2
BACK = PAIRS + 1
HALF = HEAD // 2
NT = (((1,), (1,)), ((), ()))
VMEM = pl.BlockSpec(memory_space=pltpu.VMEM)
SMEM = pl.BlockSpec(memory_space=pltpu.SMEM)
ANY = pl.BlockSpec(memory_space=pl.ANY)
in_smem = functools.partial(pltpu.with_memory_space_constraint, memory_space=pltpu.SMEM)
in_vmem = functools.partial(pltpu.with_memory_space_constraint, memory_space=pltpu.VMEM)


def slots_of(routes_ref, requests):
    routes = [routes_ref[r] for r in range(requests)]
    ranks = []
    for r in range(requests):
        rank = jnp.int32(0)
        for e in range(r):
            rank = rank + jnp.where(routes[e] == routes[r], 1, 0)
        ranks.append(rank)
    return routes, ranks


def pack_queries(groups, splits, routes_ref, q_ref, out_ref, rows_ref, x_ref, sending):
    requests = q_ref.shape[0]
    routes, ranks = slots_of(routes_ref, requests)
    q = q_ref[...].astype(jnp.float32)
    for k in range(KVH):
        for h in range(PER):
            x_ref[h * requests:(h + 1) * requests, k * HEAD:(k + 1) * HEAD] = q[
                :, (k * PER + h) * HEAD:(k * PER + h + 1) * HEAD
            ]
    x = x_ref[...].astype(jnp.bfloat16)
    cols = PER * requests
    total = groups * ROWS
    row = lax.broadcasted_iota(jnp.int32, (total, cols), 0)
    col = lax.broadcasted_iota(jnp.int32, (total, cols), 1)
    wanted = jnp.full((total, cols), -1, jnp.int32)
    for r in range(requests):
        wanted = jnp.where(col % requests == r, routes[r] * CAP + ranks[r], wanted)
    pick = (row // PER == wanted) & (row % PER == col // requests)
    placed = jnp.dot(
        pick.astype(jnp.float32).astype(jnp.bfloat16), x, preferred_element_type=jnp.float32
    ).astype(jnp.bfloat16)
    for g in range(groups):
        for k in range(KVH):
            tile = placed[g * ROWS:(g + 1) * ROWS, k * HEAD:(k + 1) * HEAD]
            for t in range(splits):
                out_ref[(g * splits + t) * KVH + k] = tile
    sending.start()
    mine = requests * PER
    row = lax.broadcasted_iota(jnp.int32, (mine, cols), 0)
    col = lax.broadcasted_iota(jnp.int32, (mine, cols), 1)
    turn = (row // PER == col % requests) & (row % PER == col // requests)
    turned = jnp.dot(
        turn.astype(jnp.float32).astype(jnp.bfloat16), x, preferred_element_type=jnp.float32
    )
    for r in range(requests):
        for k in range(KVH):
            rows_ref[r, k * PER:(k + 1) * PER, :] = turned[
                r * PER:(r + 1) * PER, k * HEAD:(k + 1) * HEAD
            ]


def prepare(groups, splits, routes_in, q_in, kv_ref, out_hbm, rows_ref, routes_ref, *refs):
    blocks, (q_ref, x_ref, out_ref, sems) = refs[:5], refs[5:]
    mine = lax.axis_index("seq") % KVH
    first = [
        pltpu.make_async_copy(routes_in, routes_ref, sems.at[KVH]),
        pltpu.make_async_copy(q_in, q_ref, sems.at[KVH + 1]),
    ]
    later = []
    for j in range(KVH):
        start = pl.multiple_of(jnp.bitwise_xor(mine, j) * HEAD, HEAD)
        later.append(
            pltpu.make_async_copy(
                kv_ref.at[0, :, :, pl.ds(start, HEAD)],
                blocks[j] if j < 2 else blocks[1 + j // 2].at[j % 2],
                sems.at[j],
            )
        )
    for copy in first + later:
        copy.start()
    for copy in first:
        copy.wait()
    sending = pltpu.make_async_copy(out_ref, out_hbm, sems.at[KVH + 2])
    pack_queries(groups, splits, routes_ref, q_ref, out_ref, rows_ref, x_ref, sending)
    for copy in later:
        copy.wait()
    sending.wait()


def suffix_kernel(len_in, rows_ref, new_in, kv_in, out_ref, stat_ref, len_ref, new_ref, kv_ref, sems):
    requests = rows_ref.shape[0]
    small = [
        pltpu.make_async_copy(len_in, len_ref, sems.at[2 * requests]),
        pltpu.make_async_copy(new_in, new_ref, sems.at[2 * requests + 1]),
    ]
    cached = [
        [
            pltpu.make_async_copy(kv_in.at[r, j], kv_ref.at[r, j], sems.at[2 * r + j])
            for r in range(requests)
        ]
        for j in range(2)
    ]
    for copy in small + cached[0] + cached[1]:
        copy.start()
    lane = lax.broadcasted_iota(jnp.int32, (HEADS, HEAD), 1)
    upper = lax.broadcasted_iota(jnp.int32, (2 * PER, HEAD), 0) < PER
    wides = []
    for r in range(requests):
        q = rows_ref[r]
        wides.append([])
        for pair in range(KVH // 2):
            two = q[2 * pair * PER:2 * (pair + 1) * PER]
            wides[r].append(
                jnp.concatenate(
                    [jnp.where(upper, two, 0.0), jnp.where(upper, 0.0, two)], axis=1
                ).astype(jnp.bfloat16)
            )
    for copy in small:
        copy.wait()
    news, owns, raws = [], [], []
    for r in range(requests):
        q = rows_ref[r]
        new = new_ref[r].astype(jnp.float32)
        news.append(new)
        owns.append(
            jnp.concatenate(
                [
                    jnp.sum(
                        q[k * PER:(k + 1) * PER] * new[0:1, k * HEAD:(k + 1) * HEAD],
                        axis=1,
                        keepdims=True,
                    )
                    for k in range(KVH)
                ],
                axis=0,
            )
        )
    for r in range(requests):
        cached[0][r].wait()
        raw = jnp.concatenate(
            [
                lax.dot_general(
                    wides[r][pair],
                    kv_ref[r, 0, :, 2 * pair * HEAD:2 * (pair + 1) * HEAD],
                    NT,
                    preferred_element_type=jnp.float32,
                )
                for pair in range(KVH // 2)
            ],
            axis=0,
        )
        live = lax.broadcasted_iota(jnp.int32, raw.shape, 1) < len_ref[r]
        raws.append(jnp.where(live, raw, -jnp.inf))
    weights, own_weights = [], []
    for r in range(requests):
        top = jnp.maximum(jnp.max(raws[r], axis=1, keepdims=True), owns[r])
        weight = jnp.exp2((raws[r] - top) * (SCALE * LOG2E))
        own_weight = jnp.exp2((owns[r] - top) * (SCALE * LOG2E))
        total = jnp.sum(weight, axis=1, keepdims=True) + own_weight
        stat_ref[r] = jnp.where(lane == 0, top * SCALE, total)
        weights.append(weight.astype(jnp.bfloat16))
        own_weights.append(own_weight.astype(jnp.bfloat16).astype(jnp.float32))
    for r in range(requests):
        cached[1][r].wait()
        for pair in range(KVH // 2):
            both = jnp.dot(
                weights[r][2 * pair * PER:2 * (pair + 1) * PER],
                kv_ref[r, 1, :, 2 * pair * HEAD:2 * (pair + 1) * HEAD],
                preferred_element_type=jnp.float32,
            )
            for j in range(2):
                k = 2 * pair + j
                rows = slice(k * PER, (k + 1) * PER)
                cols = slice(k * HEAD, (k + 1) * HEAD)
                out_ref[r, rows, :] = (
                    both[j * PER:(j + 1) * PER, j * HEAD:(j + 1) * HEAD]
                    + own_weights[r][rows] * news[r][1:2, cols]
                )


def prefix_kernel(q_ref, *refs):
    parts, out_ref = refs[:-1], refs[-1]
    views = [part for part in parts[:2]]
    views += [part.at[0] for part in parts[2:5]] + [part.at[1] for part in parts[5:]]
    keys = jnp.concatenate([view[0] for view in views], axis=0)
    values = jnp.concatenate([view[1] for view in views], axis=0)
    sources = q_ref.shape[0]
    step = HEAD // ROWS
    shape = (step * ROWS, HEAD)
    diagonal = lax.broadcasted_iota(jnp.int32, shape, 0) == lax.broadcasted_iota(jnp.int32, shape, 1)
    low = lax.broadcasted_iota(jnp.int32, (1, HEAD), 1) < HALF

    def score(i):
        q = q_ref[pl.ds(i * step, step)].reshape(shape)
        return lax.dot_general(q, keys, NT, preferred_element_type=jnp.float32)

    def weigh(raw):
        top = jnp.max(raw, axis=1, keepdims=True)
        weight = jnp.exp2((raw - top) * (SCALE * LOG2E))
        total = jnp.sum(weight, axis=1, keepdims=True)
        return top, weight.astype(jnp.bfloat16), total

    def store(i, top, weight, total):
        out = jnp.dot(weight, values, preferred_element_type=jnp.float32)
        out = (out / total).astype(SEND)
        level = top * SCALE + jnp.log(total)
        level = jnp.sum(jnp.where(diagonal, level, 0.0), axis=0, keepdims=True)
        first = level.astype(SEND).astype(jnp.float32)
        rest = level - first
        second = rest.astype(SEND).astype(jnp.float32)
        third = rest - second
        turned = [pltpu.roll(piece, HALF, 1) for piece in (first, second, third)]
        halves = [
            jnp.concatenate([jnp.where(low, first, turned[1]), third], axis=0).astype(SEND),
            jnp.concatenate([jnp.where(low, turned[0], second), turned[2]], axis=0).astype(SEND),
        ]
        for s in range(step):
            at = (i * step + s) * BACK
            out_ref[pl.ds(at, PAIRS)] = out[s * ROWS:(s + 1) * ROWS].reshape(PAIRS, 2, HEAD)
            out_ref[at + PAIRS] = halves[s // (step // 2)]

    def several(start, count):
        ahead, done = score(start), None
        for i in range(count):
            raw = ahead
            if i + 1 < count:
                ahead = score(start + i + 1)
            ready = weigh(raw)
            if done is not None:
                store(start + i - 1, *done)
            done = ready
        store(start + count - 1, *done)

    blocks = sources // step
    count = 4 if blocks % 4 == 0 else 1
    if blocks == count:
        several(0, count)
    else:
        lax.fori_loop(0, blocks // count, lambda i, c: (several(i * count, count), c)[1], 0)


def join_kernel(splits, routes_ref, back_ref, suffix_ref, stat_ref, out_ref):
    requests = out_ref.shape[0]
    routes, ranks = slots_of(routes_ref, requests)
    step = HEAD // ROWS // 2
    place = lax.axis_index("seq") % step * ROWS
    lane = lax.broadcasted_iota(jnp.int32, (PER, HEAD), 1)
    head = lax.broadcasted_iota(jnp.int32, (PER, HEAD), 0)
    pieces = [[None] * requests for _ in range(KVH)]
    for r in range(requests):
        stats = stat_ref[r]
        once = lane == head + (place + ranks[r] * PER)
        twice = lane % HALF == head + (place + ranks[r] * PER)
        for k in range(KVH):
            rows = slice(k * PER, (k + 1) * PER)
            levels, parts = [], []
            for t in range(splits):
                at = ((routes[r] * splits + t) * KVH + k) * BACK
                pair = back_ref[pl.ds(at + ranks[r] * (PER // 2), PER // 2)]
                parts.append(pair.reshape(PER, HEAD).astype(jnp.float32))
                stat = back_ref[at + PAIRS].astype(jnp.float32)
                stat = jnp.where(twice, stat[0:1], 0.0) + jnp.where(once, stat[1:2], 0.0)
                levels.append(jnp.sum(stat, axis=1, keepdims=True))
            suffix_top = stats[rows, 0:1]
            top = suffix_top
            for level in levels:
                top = jnp.maximum(top, level)
            from_suffix = jnp.exp(suffix_top - top)
            numer = from_suffix * suffix_ref[r, rows, :]
            denom = from_suffix * stats[rows, 1:2]
            for level, part in zip(levels, parts):
                from_prefix = jnp.exp(level - top)
                numer = numer + from_prefix * part
                denom = denom + from_prefix
            pieces[k][r] = numer / denom
    stacked = jnp.concatenate(
        [jnp.concatenate(pieces[k], axis=0) for k in range(KVH)], axis=1
    ).astype(jnp.bfloat16)
    mine = requests * PER
    row = lax.broadcasted_iota(jnp.int32, (PER * 8, mine), 0)
    col = lax.broadcasted_iota(jnp.int32, (PER * 8, mine), 1)
    turn = (row % 8 == col // PER) & (row // 8 == col % PER)
    turned = jnp.dot(
        turn.astype(jnp.float32).astype(jnp.bfloat16), stacked, preferred_element_type=jnp.float32
    ).astype(jnp.bfloat16)
    turned = turned.astype(jnp.float32)
    for k in range(KVH):
        for h in range(PER):
            out_ref[:, (k * PER + h) * HEAD:(k * PER + h + 1) * HEAD] = turned[
                h * 8:h * 8 + requests, k * HEAD:(k + 1) * HEAD
            ].astype(jnp.bfloat16)


def on_device(queries, new_kv, suffix_kv, suffix_len, prefix_of, prefix_kv):
    groups = lax.axis_size("grp")
    seq = lax.axis_size("seq")
    splits = seq // KVH
    requests = queries.shape[0]
    span = suffix_kv.shape[2]
    here = prefix_kv.shape[2]
    everyone = ("grp", "seq")
    routes = prefix_of.reshape(requests)

    outgoing, rows, routes, *blocks = pl.pallas_call(
        functools.partial(prepare, groups, splits),
        out_shape=[
            jax.ShapeDtypeStruct((groups * seq, ROWS, HEAD), jnp.bfloat16),
            pltpu.VMEM((requests, HEADS, HEAD), jnp.float32),
            pltpu.SMEM((requests,), jnp.int32),
        ]
        + [pltpu.VMEM((2, here, HEAD), jnp.bfloat16)] * 2
        + [pltpu.VMEM((2, 2, here, HEAD), jnp.bfloat16)] * 3,
        in_specs=[ANY, ANY, ANY],
        out_specs=[ANY, VMEM, SMEM] + [VMEM] * 5,
        scratch_shapes=[
            pltpu.VMEM((requests, HEADS * HEAD), jnp.bfloat16),
            pltpu.VMEM((PER * requests, KVH * HEAD), jnp.float32),
            pltpu.VMEM((groups * seq, ROWS, HEAD), jnp.bfloat16),
            pltpu.SemaphoreType.DMA((KVH + 3,)),
        ],
        name="prepare",
    )(routes, queries, prefix_kv)
    def swap(block, j):
        return lax.ppermute(block, "seq", [(s, s ^ j) for s in range(seq)])

    parts = [blocks[0], swap(blocks[1], 1)]
    pairs = [swap(blocks[1 + j // 2], j) for j in (6, 4, 2)]
    parts += pairs + [swap(pair, 1) for pair in pairs]

    arrived = lax.all_to_all(
        outgoing, everyone, split_axis=0, concat_axis=0, tiled=True
    )

    suffix_out, suffix_stat = pl.pallas_call(
        suffix_kernel,
        out_shape=(
            pltpu.VMEM((requests, HEADS, HEAD), jnp.float32),
            pltpu.VMEM((requests, HEADS, HEAD), jnp.float32),
        ),
        in_specs=[ANY, VMEM, ANY, ANY],
        out_specs=(VMEM, VMEM),
        scratch_shapes=[
            pltpu.SMEM((requests,), jnp.int32),
            pltpu.VMEM(new_kv.shape, jnp.bfloat16),
            pltpu.VMEM(suffix_kv.shape, jnp.bfloat16),
            pltpu.SemaphoreType.DMA((2 * requests + 2,)),
        ],
        cost_estimate=pl.CostEstimate(
            flops=4 * requests * HEADS * KVH * HEAD * span,
            bytes_accessed=2 * suffix_kv.size,
            transcendentals=requests * HEADS * span,
        ),
        name="suffix_attention",
    )(suffix_len, in_vmem(rows), new_kv, suffix_kv)

    arrived, suffix_out, suffix_stat = lax.optimization_barrier(
        (arrived, suffix_out, suffix_stat)
    )

    back = pl.pallas_call(
        prefix_kernel,
        out_shape=pltpu.VMEM((groups * seq * BACK, 2, HEAD), SEND),
        in_specs=[VMEM] * (1 + KVH),
        out_specs=VMEM,
        compiler_params=pltpu.CompilerParams(vmem_limit_bytes=32 * 1024 * 1024),
        name="prefix_attention",
    )(arrived, *parts)

    home = in_vmem(lax.all_to_all(back, everyone, split_axis=0, concat_axis=0, tiled=True))

    return pl.pallas_call(
        functools.partial(join_kernel, splits),
        out_shape=jax.ShapeDtypeStruct((requests, HEADS * HEAD), jnp.bfloat16),
        in_specs=[SMEM, VMEM, VMEM, VMEM],
        out_specs=VMEM,
        name="join",
    )(in_smem(routes), home, in_vmem(suffix_out), in_vmem(suffix_stat))


def solution(mesh):
    in_specs = (
        P(("grp", "seq"), None),
        P(("grp", "seq"), None, None),
        P(("grp", "seq"), None, None, None),
        P(("grp", "seq")),
        P(("grp", "seq"), None),
        P("grp", None, "seq", None),
    )
    out_specs = P(("grp", "seq"), None)
    return jax.shard_map(
        on_device, mesh=mesh, in_specs=in_specs, out_specs=out_specs, check_vma=False
    )
```

```python
import functools
import math

import jax
import jax.numpy as jnp
from jax import lax
from jax.experimental import pallas as pl
from jax.experimental.pallas import tpu as pltpu
from jax.sharding import PartitionSpec as P

HEADS = 64
KVH = 8
HEAD = 128
CAP = 2
PER = HEADS // KVH
SCALE = HEAD ** (-0.5)
LOG2E = math.log2(math.e)
LN2 = math.log(2.0)
SEND = jnp.bfloat16
ROWS = CAP * PER
PAIRS = ROWS // 2
BACK = PAIRS + 1
HALF = HEAD // 2
NT = (((1,), (1,)), ((), ()))
VMEM = pl.BlockSpec(memory_space=pltpu.VMEM)
SMEM = pl.BlockSpec(memory_space=pltpu.SMEM)
ANY = pl.BlockSpec(memory_space=pl.ANY)
in_smem = functools.partial(pltpu.with_memory_space_constraint, memory_space=pltpu.SMEM)
in_vmem = functools.partial(pltpu.with_memory_space_constraint, memory_space=pltpu.VMEM)


def position(g, s, groups, seq):
    return s * groups + (groups - 1 - g)


def slots_of(routes_ref, requests):
    routes = [routes_ref[r] for r in range(requests)]
    ranks = []
    for r in range(requests):
        rank = jnp.int32(0)
        for e in range(r):
            rank = rank + jnp.where(routes[e] == routes[r], 1, 0)
        ranks.append(rank)
    return routes, ranks


def pack_queries(groups, splits, routes_ref, q_ref, out_ref, rows_ref, x_ref, sending):
    requests = q_ref.shape[0]
    routes, ranks = slots_of(routes_ref, requests)
    q = q_ref[...].astype(jnp.float32)
    for k in range(KVH):
        for h in range(PER):
            x_ref[h * requests:(h + 1) * requests, k * HEAD:(k + 1) * HEAD] = q[
                :, (k * PER + h) * HEAD:(k * PER + h + 1) * HEAD
            ]
    x = x_ref[...].astype(jnp.bfloat16)
    cols = PER * requests
    total = groups * ROWS
    row = lax.broadcasted_iota(jnp.int32, (total, cols), 0)
    col = lax.broadcasted_iota(jnp.int32, (total, cols), 1)
    wanted = jnp.full((total, cols), -1, jnp.int32)
    for r in range(requests):
        wanted = jnp.where(col % requests == r, routes[r] * CAP + ranks[r], wanted)
    pick = (row // PER == wanted) & (row % PER == col // requests)
    placed = jnp.dot(
        pick.astype(jnp.float32).astype(jnp.bfloat16), x, preferred_element_type=jnp.float32
    ).astype(jnp.bfloat16)
    for g in range(groups):
        for k in range(KVH):
            tile = placed[g * ROWS:(g + 1) * ROWS, k * HEAD:(k + 1) * HEAD]
            for t in range(splits):
                out_ref[position(g, t * KVH + k, groups, splits * KVH)] = tile
    sending.start()
    mine = requests * PER
    row = lax.broadcasted_iota(jnp.int32, (mine, cols), 0)
    col = lax.broadcasted_iota(jnp.int32, (mine, cols), 1)
    turn = (row // PER == col % requests) & (row % PER == col // requests)
    turned = jnp.dot(
        turn.astype(jnp.float32).astype(jnp.bfloat16), x, preferred_element_type=jnp.float32
    )
    for r in range(requests):
        for k in range(KVH):
            rows_ref[r, k * PER:(k + 1) * PER, :] = turned[
                r * PER:(r + 1) * PER, k * HEAD:(k + 1) * HEAD
            ]


def prepare(groups, splits, routes_in, q_in, kv_ref, out_hbm, rows_ref, routes_ref, *refs):
    blocks, (q_ref, x_ref, out_ref, sems) = refs[:5], refs[5:]
    mine = lax.axis_index("seq") % KVH
    first = [
        pltpu.make_async_copy(routes_in, routes_ref, sems.at[KVH]),
        pltpu.make_async_copy(q_in, q_ref, sems.at[KVH + 1]),
    ]
    later = []
    for j in range(KVH):
        start = pl.multiple_of(jnp.bitwise_xor(mine, j) * HEAD, HEAD)
        later.append(
            pltpu.make_async_copy(
                kv_ref.at[0, :, :, pl.ds(start, HEAD)],
                blocks[j] if j < 2 else blocks[1 + j // 2].at[j % 2],
                sems.at[j],
            )
        )
    for copy in first + later:
        copy.start()
    for copy in first:
        copy.wait()
    sending = pltpu.make_async_copy(out_ref, out_hbm, sems.at[KVH + 2])
    pack_queries(groups, splits, routes_ref, q_ref, out_ref, rows_ref, x_ref, sending)
    for copy in later:
        copy.wait()
    sending.wait()


def suffix_kernel(len_in, rows_ref, new_in, kv_in, out_ref, stat_ref, len_ref, new_ref, kv_ref, sems):
    requests = rows_ref.shape[0]
    small = [
        pltpu.make_async_copy(len_in, len_ref, sems.at[2 * requests]),
        pltpu.make_async_copy(new_in, new_ref, sems.at[2 * requests + 1]),
    ]
    cached = [
        [
            pltpu.make_async_copy(kv_in.at[r, j], kv_ref.at[r, j], sems.at[2 * r + j])
            for r in range(requests)
        ]
        for j in range(2)
    ]
    for copy in small + cached[0] + cached[1]:
        copy.start()
    lane = lax.broadcasted_iota(jnp.int32, (HEADS, HEAD), 1)
    upper = lax.broadcasted_iota(jnp.int32, (2 * PER, HEAD), 0) < PER
    wides = []
    for r in range(requests):
        q = rows_ref[r]
        wides.append([])
        for pair in range(KVH // 2):
            two = q[2 * pair * PER:2 * (pair + 1) * PER]
            wides[r].append(
                jnp.concatenate(
                    [jnp.where(upper, two, 0.0), jnp.where(upper, 0.0, two)], axis=1
                ).astype(jnp.bfloat16)
            )
    for copy in small:
        copy.wait()
    news, owns, raws = [], [], []
    for r in range(requests):
        q = rows_ref[r]
        new = new_ref[r].astype(jnp.float32)
        news.append(new)
        owns.append(
            jnp.concatenate(
                [
                    jnp.sum(
                        q[k * PER:(k + 1) * PER] * new[0:1, k * HEAD:(k + 1) * HEAD],
                        axis=1,
                        keepdims=True,
                    )
                    for k in range(KVH)
                ],
                axis=0,
            )
        )
    for r in range(requests):
        cached[0][r].wait()
        raw = jnp.concatenate(
            [
                lax.dot_general(
                    wides[r][pair],
                    kv_ref[r, 0, :, 2 * pair * HEAD:2 * (pair + 1) * HEAD],
                    NT,
                    preferred_element_type=jnp.float32,
                )
                for pair in range(KVH // 2)
            ],
            axis=0,
        )
        live = lax.broadcasted_iota(jnp.int32, raw.shape, 1) < len_ref[r]
        raws.append(jnp.where(live, raw, -jnp.inf))
    weights, own_weights = [], []
    for r in range(requests):
        top = jnp.maximum(jnp.max(raws[r], axis=1, keepdims=True), owns[r])
        weight = jnp.exp2((raws[r] - top) * (SCALE * LOG2E))
        own_weight = jnp.exp2((owns[r] - top) * (SCALE * LOG2E))
        total = jnp.sum(weight, axis=1, keepdims=True) + own_weight
        stat_ref[r] = jnp.where(lane == 0, top * SCALE, total)
        weights.append(weight.astype(jnp.bfloat16))
        own_weights.append(own_weight.astype(jnp.bfloat16).astype(jnp.float32))
    for r in range(requests):
        cached[1][r].wait()
        for pair in range(KVH // 2):
            both = jnp.dot(
                weights[r][2 * pair * PER:2 * (pair + 1) * PER],
                kv_ref[r, 1, :, 2 * pair * HEAD:2 * (pair + 1) * HEAD],
                preferred_element_type=jnp.float32,
            )
            for j in range(2):
                k = 2 * pair + j
                rows = slice(k * PER, (k + 1) * PER)
                cols = slice(k * HEAD, (k + 1) * HEAD)
                out_ref[r, rows, :] = (
                    both[j * PER:(j + 1) * PER, j * HEAD:(j + 1) * HEAD]
                    + own_weights[r][rows] * news[r][1:2, cols]
                )


def prefix_kernel(q_ref, *refs):
    parts, out_ref = refs[:-1], refs[-1]
    views = [part for part in parts[:2]]
    views += [part.at[0] for part in parts[2:5]] + [part.at[1] for part in parts[5:]]
    keys = jnp.concatenate([view[0] for view in views], axis=0)
    values = jnp.concatenate([view[1] for view in views], axis=0)
    sources = q_ref.shape[0]
    step = HEAD // ROWS
    shape = (step * ROWS, HEAD)
    diagonal = lax.broadcasted_iota(jnp.int32, shape, 0) == lax.broadcasted_iota(jnp.int32, shape, 1)
    low = lax.broadcasted_iota(jnp.int32, (1, HEAD), 1) < HALF

    def score(i):
        q = q_ref[pl.ds(i * step, step)].reshape(shape)
        return lax.dot_general(q, keys, NT, preferred_element_type=jnp.float32)

    def weigh(raw):
        top = jnp.max(raw, axis=1, keepdims=True)
        weight = jnp.exp2((raw - top) * (SCALE * LOG2E))
        total = jnp.sum(weight, axis=1, keepdims=True)
        return top, weight.astype(jnp.bfloat16), total

    def store(i, top, weight, total):
        out = jnp.dot(weight, values, preferred_element_type=jnp.float32)
        out = (out / total).astype(SEND)
        level = top * SCALE + jnp.log(total)
        level = jnp.sum(jnp.where(diagonal, level, 0.0), axis=0, keepdims=True)
        first = level.astype(SEND).astype(jnp.float32)
        rest = level - first
        second = rest.astype(SEND).astype(jnp.float32)
        third = rest - second
        turned = [pltpu.roll(piece, HALF, 1) for piece in (first, second, third)]
        halves = [
            jnp.concatenate([jnp.where(low, first, turned[1]), third], axis=0).astype(SEND),
            jnp.concatenate([jnp.where(low, turned[0], second), turned[2]], axis=0).astype(SEND),
        ]
        for s in range(step):
            at = (i * step + s) * BACK
            out_ref[pl.ds(at, PAIRS)] = out[s * ROWS:(s + 1) * ROWS].reshape(PAIRS, 2, HEAD)
            out_ref[at + PAIRS] = halves[s // (step // 2)]

    def several(start, count):
        ahead, done = score(start), None
        for i in range(count):
            raw = ahead
            if i + 1 < count:
                ahead = score(start + i + 1)
            ready = weigh(raw)
            if done is not None:
                store(start + i - 1, *done)
            done = ready
        store(start + count - 1, *done)

    blocks = sources // step
    count = 4 if blocks % 4 == 0 else 1
    if blocks == count:
        several(0, count)
    else:
        lax.fori_loop(0, blocks // count, lambda i, c: (several(i * count, count), c)[1], 0)


def join_kernel(splits, routes_ref, back_ref, suffix_ref, stat_ref, out_ref):
    requests = out_ref.shape[0]
    routes, ranks = slots_of(routes_ref, requests)
    step = HEAD // ROWS // 2
    place = position(lax.axis_index("grp"), lax.axis_index("seq"), lax.axis_size("grp"), lax.axis_size("seq")) % step * ROWS
    lane = lax.broadcasted_iota(jnp.int32, (PER, HEAD), 1)
    head = lax.broadcasted_iota(jnp.int32, (PER, HEAD), 0)
    pieces = [[None] * requests for _ in range(KVH)]
    for r in range(requests):
        stats = stat_ref[r]
        once = lane == head + (place + ranks[r] * PER)
        twice = lane % HALF == head + (place + ranks[r] * PER)
        for k in range(KVH):
            rows = slice(k * PER, (k + 1) * PER)
            levels, parts = [], []
            for t in range(splits):
                at = position(routes[r], t * KVH + k, lax.axis_size("grp"), splits * KVH) * BACK
                pair = back_ref[pl.ds(at + ranks[r] * (PER // 2), PER // 2)]
                parts.append(pair.reshape(PER, HEAD).astype(jnp.float32))
                stat = back_ref[at + PAIRS].astype(jnp.float32)
                stat = jnp.where(twice, stat[0:1], 0.0) + jnp.where(once, stat[1:2], 0.0)
                levels.append(jnp.sum(stat, axis=1, keepdims=True))
            suffix_top = stats[rows, 0:1]
            top = suffix_top
            for level in levels:
                top = jnp.maximum(top, level)
            from_suffix = jnp.exp(suffix_top - top)
            numer = from_suffix * suffix_ref[r, rows, :]
            denom = from_suffix * stats[rows, 1:2]
            for level, part in zip(levels, parts):
                from_prefix = jnp.exp(level - top)
                numer = numer + from_prefix * part
                denom = denom + from_prefix
            pieces[k][r] = numer / denom
    stacked = jnp.concatenate(
        [jnp.concatenate(pieces[k], axis=0) for k in range(KVH)], axis=1
    ).astype(jnp.bfloat16)
    mine = requests * PER
    row = lax.broadcasted_iota(jnp.int32, (PER * 8, mine), 0)
    col = lax.broadcasted_iota(jnp.int32, (PER * 8, mine), 1)
    turn = (row % 8 == col // PER) & (row // 8 == col % PER)
    turned = jnp.dot(
        turn.astype(jnp.float32).astype(jnp.bfloat16), stacked, preferred_element_type=jnp.float32
    ).astype(jnp.bfloat16)
    turned = turned.astype(jnp.float32)
    for k in range(KVH):
        for h in range(PER):
            out_ref[:, (k * PER + h) * HEAD:(k * PER + h + 1) * HEAD] = turned[
                h * 8:h * 8 + requests, k * HEAD:(k + 1) * HEAD
            ].astype(jnp.bfloat16)


def on_device(queries, new_kv, suffix_kv, suffix_len, prefix_of, prefix_kv):
    groups = lax.axis_size("grp")
    seq = lax.axis_size("seq")
    splits = seq // KVH
    requests = queries.shape[0]
    span = suffix_kv.shape[2]
    here = prefix_kv.shape[2]
    everyone = ("grp", "seq")
    order = [0] * (groups * seq)
    for g in range(groups):
        for s in range(seq):
            order[position(g, s, groups, seq)] = g * seq + s
    routes = prefix_of.reshape(requests)

    outgoing, rows, routes, *blocks = pl.pallas_call(
        functools.partial(prepare, groups, splits),
        out_shape=[
            jax.ShapeDtypeStruct((groups * seq, ROWS, HEAD), jnp.bfloat16),
            pltpu.VMEM((requests, HEADS, HEAD), jnp.float32),
            pltpu.SMEM((requests,), jnp.int32),
        ]
        + [pltpu.VMEM((2, here, HEAD), jnp.bfloat16)] * 2
        + [pltpu.VMEM((2, 2, here, HEAD), jnp.bfloat16)] * 3,
        in_specs=[ANY, ANY, ANY],
        out_specs=[ANY, VMEM, SMEM] + [VMEM] * 5,
        scratch_shapes=[
            pltpu.VMEM((requests, HEADS * HEAD), jnp.bfloat16),
            pltpu.VMEM((PER * requests, KVH * HEAD), jnp.float32),
            pltpu.VMEM((groups * seq, ROWS, HEAD), jnp.bfloat16),
            pltpu.SemaphoreType.DMA((KVH + 3,)),
        ],
        name="prepare",
    )(routes, queries, prefix_kv)
    def swap(block, j):
        return lax.ppermute(block, "seq", [(s, s ^ j) for s in range(seq)])

    parts = [blocks[0], swap(blocks[1], 1)]
    pairs = [swap(blocks[1 + j // 2], j) for j in (6, 4, 2)]
    parts += pairs + [swap(pair, 1) for pair in pairs]

    arrived = lax.all_to_all(
        outgoing, everyone, split_axis=0, concat_axis=0, tiled=True, axis_index_groups=[order]
    )

    suffix_out, suffix_stat = pl.pallas_call(
        suffix_kernel,
        out_shape=(
            pltpu.VMEM((requests, HEADS, HEAD), jnp.float32),
            pltpu.VMEM((requests, HEADS, HEAD), jnp.float32),
        ),
        in_specs=[ANY, VMEM, ANY, ANY],
        out_specs=(VMEM, VMEM),
        scratch_shapes=[
            pltpu.SMEM((requests,), jnp.int32),
            pltpu.VMEM(new_kv.shape, jnp.bfloat16),
            pltpu.VMEM(suffix_kv.shape, jnp.bfloat16),
            pltpu.SemaphoreType.DMA((2 * requests + 2,)),
        ],
        cost_estimate=pl.CostEstimate(
            flops=4 * requests * HEADS * KVH * HEAD * span,
            bytes_accessed=2 * suffix_kv.size,
            transcendentals=requests * HEADS * span,
        ),
        name="suffix_attention",
    )(suffix_len, in_vmem(rows), new_kv, suffix_kv)

    arrived, suffix_out, suffix_stat = lax.optimization_barrier(
        (arrived, suffix_out, suffix_stat)
    )

    back = pl.pallas_call(
        prefix_kernel,
        out_shape=pltpu.VMEM((groups * seq * BACK, 2, HEAD), SEND),
        in_specs=[VMEM] * (1 + KVH),
        out_specs=VMEM,
        compiler_params=pltpu.CompilerParams(vmem_limit_bytes=32 * 1024 * 1024),
        name="prefix_attention",
    )(arrived, *parts)

    home = in_vmem(
        lax.all_to_all(
            back, everyone, split_axis=0, concat_axis=0, tiled=True, axis_index_groups=[order]
        )
    )

    return pl.pallas_call(
        functools.partial(join_kernel, splits),
        out_shape=jax.ShapeDtypeStruct((requests, HEADS * HEAD), jnp.bfloat16),
        in_specs=[SMEM, VMEM, VMEM, VMEM],
        out_specs=VMEM,
        name="join",
    )(in_smem(routes), home, in_vmem(suffix_out), in_vmem(suffix_stat))


def solution(mesh):
    in_specs = (
        P(("grp", "seq"), None),
        P(("grp", "seq"), None, None),
        P(("grp", "seq"), None, None, None),
        P(("grp", "seq")),
        P(("grp", "seq"), None),
        P("grp", None, "seq", None),
    )
    out_specs = P(("grp", "seq"), None)
    return jax.shard_map(
        on_device, mesh=mesh, in_specs=in_specs, out_specs=out_specs, check_vma=False
    )
```

```python
import functools
import math

import jax
import jax.numpy as jnp
from jax import lax
from jax.experimental import pallas as pl
from jax.experimental.pallas import tpu as pltpu
from jax.sharding import PartitionSpec as P

HEADS = 64
KVH = 8
HEAD = 128
CAP = 2
PER = HEADS // KVH
SCALE = HEAD ** (-0.5)
LOG2E = math.log2(math.e)
LN2 = math.log(2.0)
ROWS = CAP * PER
PAIRS = ROWS // 2
BACK = PAIRS + 1
HALF = HEAD // 2
NT = (((1,), (1,)), ((), ()))
VMEM = pl.BlockSpec(memory_space=pltpu.VMEM)
SMEM = pl.BlockSpec(memory_space=pltpu.SMEM)
ANY = pl.BlockSpec(memory_space=pl.ANY)
in_smem = functools.partial(pltpu.with_memory_space_constraint, memory_space=pltpu.SMEM)
in_vmem = functools.partial(pltpu.with_memory_space_constraint, memory_space=pltpu.VMEM)


def position(g, s, groups, seq):
    return s * groups + (groups - 1 - g)


def slots_of(routes_ref, requests):
    routes = [routes_ref[r] for r in range(requests)]
    ranks = []
    for r in range(requests):
        rank = jnp.int32(0)
        for e in range(r):
            rank = rank + jnp.where(routes[e] == routes[r], 1, 0)
        ranks.append(rank)
    return routes, ranks


def pack_queries(groups, splits, routes_ref, q_ref, out_ref, rows_ref, x_ref, sending):
    requests = q_ref.shape[0]
    routes, ranks = slots_of(routes_ref, requests)
    q = q_ref[...].astype(jnp.float32)
    for k in range(KVH):
        for h in range(PER):
            x_ref[h * requests:(h + 1) * requests, k * HEAD:(k + 1) * HEAD] = q[
                :, (k * PER + h) * HEAD:(k * PER + h + 1) * HEAD
            ]
    x = x_ref[...].astype(jnp.bfloat16)
    cols = PER * requests
    total = groups * ROWS
    row = lax.broadcasted_iota(jnp.int32, (total, cols), 0)
    col = lax.broadcasted_iota(jnp.int32, (total, cols), 1)
    wanted = jnp.full((total, cols), -1, jnp.int32)
    for r in range(requests):
        wanted = jnp.where(col % requests == r, routes[r] * CAP + ranks[r], wanted)
    pick = (row // PER == wanted) & (row % PER == col // requests)
    placed = jnp.dot(
        pick.astype(jnp.float32).astype(jnp.bfloat16), x, preferred_element_type=jnp.float32
    ).astype(jnp.bfloat16)
    for g in range(groups):
        for k in range(KVH):
            tile = placed[g * ROWS:(g + 1) * ROWS, k * HEAD:(k + 1) * HEAD]
            for t in range(splits):
                out_ref[position(g, t * KVH + k, groups, splits * KVH)] = tile
    sending.start()
    mine = requests * PER
    row = lax.broadcasted_iota(jnp.int32, (mine, cols), 0)
    col = lax.broadcasted_iota(jnp.int32, (mine, cols), 1)
    turn = (row // PER == col % requests) & (row % PER == col // requests)
    turned = jnp.dot(
        turn.astype(jnp.float32).astype(jnp.bfloat16), x, preferred_element_type=jnp.float32
    )
    for r in range(requests):
        for k in range(KVH):
            rows_ref[r, k * PER:(k + 1) * PER, :] = turned[
                r * PER:(r + 1) * PER, k * HEAD:(k + 1) * HEAD
            ]


def prepare(groups, splits, routes_in, q_in, kv_ref, out_hbm, rows_ref, routes_ref, *refs):
    blocks, (q_ref, x_ref, out_ref, sems) = refs[:5], refs[5:]
    mine = lax.axis_index("seq") % KVH
    first = [
        pltpu.make_async_copy(routes_in, routes_ref, sems.at[KVH]),
        pltpu.make_async_copy(q_in, q_ref, sems.at[KVH + 1]),
    ]
    later = []
    for j in range(KVH):
        start = pl.multiple_of(jnp.bitwise_xor(mine, j) * HEAD, HEAD)
        later.append(
            pltpu.make_async_copy(
                kv_ref.at[0, :, :, pl.ds(start, HEAD)],
                blocks[j] if j < 2 else blocks[1 + j // 2].at[j % 2],
                sems.at[j],
            )
        )
    for copy in first + later:
        copy.start()
    for copy in first:
        copy.wait()
    sending = pltpu.make_async_copy(out_ref, out_hbm, sems.at[KVH + 2])
    pack_queries(groups, splits, routes_ref, q_ref, out_ref, rows_ref, x_ref, sending)
    for copy in later:
        copy.wait()
    sending.wait()


def suffix_kernel(len_in, rows_ref, new_in, kv_in, out_ref, stat_ref, len_ref, new_ref, kv_ref, sems):
    requests = rows_ref.shape[0]
    small = [
        pltpu.make_async_copy(len_in, len_ref, sems.at[2 * requests]),
        pltpu.make_async_copy(new_in, new_ref, sems.at[2 * requests + 1]),
    ]
    cached = [
        [
            pltpu.make_async_copy(kv_in.at[r, j], kv_ref.at[r, j], sems.at[2 * r + j])
            for r in range(requests)
        ]
        for j in range(2)
    ]
    for copy in small + cached[0] + cached[1]:
        copy.start()
    lane = lax.broadcasted_iota(jnp.int32, (HEADS, HEAD), 1)
    upper = lax.broadcasted_iota(jnp.int32, (2 * PER, HEAD), 0) < PER
    wides = []
    for r in range(requests):
        q = rows_ref[r]
        wides.append([])
        for pair in range(KVH // 2):
            two = q[2 * pair * PER:2 * (pair + 1) * PER]
            wides[r].append(
                jnp.concatenate(
                    [jnp.where(upper, two, 0.0), jnp.where(upper, 0.0, two)], axis=1
                ).astype(jnp.bfloat16)
            )
    for copy in small:
        copy.wait()
    news, owns, raws = [], [], []
    for r in range(requests):
        q = rows_ref[r]
        new = new_ref[r].astype(jnp.float32)
        news.append(new)
        owns.append(
            jnp.concatenate(
                [
                    jnp.sum(
                        q[k * PER:(k + 1) * PER] * new[0:1, k * HEAD:(k + 1) * HEAD],
                        axis=1,
                        keepdims=True,
                    )
                    for k in range(KVH)
                ],
                axis=0,
            )
        )
    for r in range(requests):
        cached[0][r].wait()
        raw = jnp.concatenate(
            [
                lax.dot_general(
                    wides[r][pair],
                    kv_ref[r, 0, :, 2 * pair * HEAD:2 * (pair + 1) * HEAD],
                    NT,
                    preferred_element_type=jnp.float32,
                )
                for pair in range(KVH // 2)
            ],
            axis=0,
        )
        live = lax.broadcasted_iota(jnp.int32, raw.shape, 1) < len_ref[r]
        raws.append(jnp.where(live, raw, -jnp.inf))
    weights, own_weights = [], []
    for r in range(requests):
        top = jnp.maximum(jnp.max(raws[r], axis=1, keepdims=True), owns[r])
        weight = jnp.exp2((raws[r] - top) * (SCALE * LOG2E))
        own_weight = jnp.exp2((owns[r] - top) * (SCALE * LOG2E))
        total = jnp.sum(weight, axis=1, keepdims=True) + own_weight
        stat_ref[r] = jnp.where(lane == 0, top * SCALE, total)
        weights.append(weight.astype(jnp.bfloat16))
        own_weights.append(own_weight.astype(jnp.bfloat16).astype(jnp.float32))
    for r in range(requests):
        cached[1][r].wait()
        for pair in range(KVH // 2):
            both = jnp.dot(
                weights[r][2 * pair * PER:2 * (pair + 1) * PER],
                kv_ref[r, 1, :, 2 * pair * HEAD:2 * (pair + 1) * HEAD],
                preferred_element_type=jnp.float32,
            )
            for j in range(2):
                k = 2 * pair + j
                rows = slice(k * PER, (k + 1) * PER)
                cols = slice(k * HEAD, (k + 1) * HEAD)
                out_ref[r, rows, :] = (
                    both[j * PER:(j + 1) * PER, j * HEAD:(j + 1) * HEAD]
                    + own_weights[r][rows] * news[r][1:2, cols]
                )


def prefix_kernel(splits, q_ref, *refs):
    parts, out_ref = refs[:-1], refs[-1]
    send = out_ref.dtype
    views = [part for part in parts[:2]]
    views += [part.at[0] for part in parts[2:5]] + [part.at[1] for part in parts[5:]]
    keys = jnp.concatenate([view[0] for view in views], axis=0)
    values = jnp.concatenate([view[1] for view in views], axis=0)
    sources = q_ref.shape[0]
    step = HEAD // ROWS
    shape = (step * ROWS, HEAD)
    diagonal = lax.broadcasted_iota(jnp.int32, shape, 0) == lax.broadcasted_iota(jnp.int32, shape, 1)
    low = lax.broadcasted_iota(jnp.int32, (1, HEAD), 1) < HALF

    def score(i):
        q = q_ref[pl.ds(i * step, step)].reshape(shape)
        return lax.dot_general(q, keys, NT, preferred_element_type=jnp.float32)

    def weigh(raw):
        top = jnp.max(raw, axis=1, keepdims=True)
        weight = jnp.exp2((raw - top) * (SCALE * LOG2E))
        total = jnp.sum(weight, axis=1, keepdims=True)
        rounded = weight.astype(jnp.bfloat16)
        if splits == 1:
            return top, (rounded,), total
        return top, (rounded, (weight - rounded.astype(jnp.float32)).astype(jnp.bfloat16)), total

    def store(i, top, weights, total):
        out = sum(jnp.dot(w, values, preferred_element_type=jnp.float32) for w in weights)
        out = (out / total).astype(send)
        level = top * SCALE + jnp.log(total)
        level = jnp.sum(jnp.where(diagonal, level, 0.0), axis=0, keepdims=True)
        first = level.astype(send).astype(jnp.float32)
        rest = level - first
        second = rest.astype(send).astype(jnp.float32)
        third = rest - second
        turned = [pltpu.roll(piece, HALF, 1) for piece in (first, second, third)]
        halves = [
            jnp.concatenate([jnp.where(low, first, turned[1]), third], axis=0).astype(send),
            jnp.concatenate([jnp.where(low, turned[0], second), turned[2]], axis=0).astype(send),
        ]
        for s in range(step):
            at = (i * step + s) * BACK
            out_ref[pl.ds(at, PAIRS)] = out[s * ROWS:(s + 1) * ROWS].reshape(PAIRS, 2, HEAD)
            out_ref[at + PAIRS] = halves[s // (step // 2)]

    def several(start, count):
        ahead, done = score(start), None
        for i in range(count):
            raw = ahead
            if i + 1 < count:
                ahead = score(start + i + 1)
            ready = weigh(raw)
            if done is not None:
                store(start + i - 1, *done)
            done = ready
        store(start + count - 1, *done)

    blocks = sources // step
    count = 4 if blocks % 4 == 0 else 1
    if blocks == count:
        several(0, count)
    else:
        lax.fori_loop(0, blocks // count, lambda i, c: (several(i * count, count), c)[1], 0)


def join_kernel(splits, routes_ref, back_ref, suffix_ref, stat_ref, out_ref):
    requests = out_ref.shape[0]
    routes, ranks = slots_of(routes_ref, requests)
    step = HEAD // ROWS // 2
    place = position(lax.axis_index("grp"), lax.axis_index("seq"), lax.axis_size("grp"), lax.axis_size("seq")) % step * ROWS
    lane = lax.broadcasted_iota(jnp.int32, (PER, HEAD), 1)
    head = lax.broadcasted_iota(jnp.int32, (PER, HEAD), 0)
    pieces = [[None] * requests for _ in range(KVH)]
    for r in range(requests):
        stats = stat_ref[r]
        once = lane == head + (place + ranks[r] * PER)
        twice = lane % HALF == head + (place + ranks[r] * PER)
        for k in range(KVH):
            rows = slice(k * PER, (k + 1) * PER)
            levels, parts = [], []
            for t in range(splits):
                at = position(routes[r], t * KVH + k, lax.axis_size("grp"), splits * KVH) * BACK
                pair = back_ref[pl.ds(at + ranks[r] * (PER // 2), PER // 2)]
                parts.append(pair.reshape(PER, HEAD).astype(jnp.float32))
                stat = back_ref[at + PAIRS].astype(jnp.float32)
                stat = jnp.where(twice, stat[0:1], 0.0) + jnp.where(once, stat[1:2], 0.0)
                levels.append(jnp.sum(stat, axis=1, keepdims=True))
            suffix_top = stats[rows, 0:1]
            top = suffix_top
            for level in levels:
                top = jnp.maximum(top, level)
            from_suffix = jnp.exp(suffix_top - top)
            numer = from_suffix * suffix_ref[r, rows, :]
            denom = from_suffix * stats[rows, 1:2]
            for level, part in zip(levels, parts):
                from_prefix = jnp.exp(level - top)
                numer = numer + from_prefix * part
                denom = denom + from_prefix
            pieces[k][r] = numer / denom
    stacked = jnp.concatenate(
        [jnp.concatenate(pieces[k], axis=0) for k in range(KVH)], axis=1
    ).astype(jnp.bfloat16)
    mine = requests * PER
    row = lax.broadcasted_iota(jnp.int32, (PER * 8, mine), 0)
    col = lax.broadcasted_iota(jnp.int32, (PER * 8, mine), 1)
    turn = (row % 8 == col // PER) & (row // 8 == col % PER)
    turned = jnp.dot(
        turn.astype(jnp.float32).astype(jnp.bfloat16), stacked, preferred_element_type=jnp.float32
    ).astype(jnp.bfloat16)
    turned = turned.astype(jnp.float32)
    for k in range(KVH):
        for h in range(PER):
            out_ref[:, (k * PER + h) * HEAD:(k * PER + h + 1) * HEAD] = turned[
                h * 8:h * 8 + requests, k * HEAD:(k + 1) * HEAD
            ].astype(jnp.bfloat16)


def on_device(queries, new_kv, suffix_kv, suffix_len, prefix_of, prefix_kv):
    groups = lax.axis_size("grp")
    seq = lax.axis_size("seq")
    splits = seq // KVH
    requests = queries.shape[0]
    span = suffix_kv.shape[2]
    here = prefix_kv.shape[2]
    everyone = ("grp", "seq")
    order = [0] * (groups * seq)
    for g in range(groups):
        for s in range(seq):
            order[position(g, s, groups, seq)] = g * seq + s
    routes = prefix_of.reshape(requests)

    outgoing, rows, routes, *blocks = pl.pallas_call(
        functools.partial(prepare, groups, splits),
        out_shape=[
            jax.ShapeDtypeStruct((groups * seq, ROWS, HEAD), jnp.bfloat16),
            pltpu.VMEM((requests, HEADS, HEAD), jnp.float32),
            pltpu.SMEM((requests,), jnp.int32),
        ]
        + [pltpu.VMEM((2, here, HEAD), jnp.bfloat16)] * 2
        + [pltpu.VMEM((2, 2, here, HEAD), jnp.bfloat16)] * 3,
        in_specs=[ANY, ANY, ANY],
        out_specs=[ANY, VMEM, SMEM] + [VMEM] * 5,
        scratch_shapes=[
            pltpu.VMEM((requests, HEADS * HEAD), jnp.bfloat16),
            pltpu.VMEM((PER * requests, KVH * HEAD), jnp.float32),
            pltpu.VMEM((groups * seq, ROWS, HEAD), jnp.bfloat16),
            pltpu.SemaphoreType.DMA((KVH + 3,)),
        ],
        name="prepare",
    )(routes, queries, prefix_kv)
    def swap(block, j):
        return lax.ppermute(block, "seq", [(s, s ^ j) for s in range(seq)])

    parts = [blocks[0], swap(blocks[1], 1)]
    pairs = [swap(blocks[1 + j // 2], j) for j in (6, 4, 2)]
    parts += pairs + [swap(pair, 1) for pair in pairs]

    arrived = lax.all_to_all(
        outgoing, everyone, split_axis=0, concat_axis=0, tiled=True, axis_index_groups=[order]
    )

    suffix_out, suffix_stat = pl.pallas_call(
        suffix_kernel,
        out_shape=(
            pltpu.VMEM((requests, HEADS, HEAD), jnp.float32),
            pltpu.VMEM((requests, HEADS, HEAD), jnp.float32),
        ),
        in_specs=[ANY, VMEM, ANY, ANY],
        out_specs=(VMEM, VMEM),
        scratch_shapes=[
            pltpu.SMEM((requests,), jnp.int32),
            pltpu.VMEM(new_kv.shape, jnp.bfloat16),
            pltpu.VMEM(suffix_kv.shape, jnp.bfloat16),
            pltpu.SemaphoreType.DMA((2 * requests + 2,)),
        ],
        cost_estimate=pl.CostEstimate(
            flops=4 * requests * HEADS * KVH * HEAD * span,
            bytes_accessed=2 * suffix_kv.size,
            transcendentals=requests * HEADS * span,
        ),
        name="suffix_attention",
    )(suffix_len, in_vmem(rows), new_kv, suffix_kv)

    arrived, suffix_out, suffix_stat = lax.optimization_barrier(
        (arrived, suffix_out, suffix_stat)
    )

    send = jnp.bfloat16 if splits == 1 else jnp.float32
    back = pl.pallas_call(
        functools.partial(prefix_kernel, splits),
        out_shape=pltpu.VMEM((groups * seq * BACK, 2, HEAD), send),
        in_specs=[VMEM] * (1 + KVH),
        out_specs=VMEM,
        compiler_params=pltpu.CompilerParams(vmem_limit_bytes=32 * 1024 * 1024),
        name="prefix_attention",
    )(arrived, *parts)

    home = in_vmem(
        lax.all_to_all(
            back, everyone, split_axis=0, concat_axis=0, tiled=True, axis_index_groups=[order]
        )
    )

    return pl.pallas_call(
        functools.partial(join_kernel, splits),
        out_shape=jax.ShapeDtypeStruct((requests, HEADS * HEAD), jnp.bfloat16),
        in_specs=[SMEM, VMEM, VMEM, VMEM],
        out_specs=VMEM,
        name="join",
    )(in_smem(routes), home, in_vmem(suffix_out), in_vmem(suffix_stat))


def solution(mesh):
    in_specs = (
        P(("grp", "seq"), None),
        P(("grp", "seq"), None, None),
        P(("grp", "seq"), None, None, None),
        P(("grp", "seq")),
        P(("grp", "seq"), None),
        P("grp", None, "seq", None),
    )
    out_specs = P(("grp", "seq"), None)
    return jax.shard_map(
        on_device, mesh=mesh, in_specs=in_specs, out_specs=out_specs, check_vma=False
    )
```

```python
import functools
import math

import jax
import jax.numpy as jnp
from jax import lax
from jax.experimental import pallas as pl
from jax.experimental.pallas import tpu as pltpu
from jax.sharding import PartitionSpec as P

HEADS = 64
KVH = 8
HEAD = 128
CAP = 2
PER = HEADS // KVH
SCALE = HEAD ** (-0.5)
LOG2E = math.log2(math.e)
LN2 = math.log(2.0)
ROWS = CAP * PER
PAIRS = ROWS // 2
BACK = PAIRS + 1
HALF = HEAD // 2
NT = (((1,), (1,)), ((), ()))
VMEM = pl.BlockSpec(memory_space=pltpu.VMEM)
SMEM = pl.BlockSpec(memory_space=pltpu.SMEM)
ANY = pl.BlockSpec(memory_space=pl.ANY)
in_smem = functools.partial(pltpu.with_memory_space_constraint, memory_space=pltpu.SMEM)
in_vmem = functools.partial(pltpu.with_memory_space_constraint, memory_space=pltpu.VMEM)


def position(g, s, groups, seq):
    return s * groups + (groups - 1 - g)


def slots_of(routes_ref, requests):
    routes = [routes_ref[r] for r in range(requests)]
    ranks = []
    for r in range(requests):
        rank = jnp.int32(0)
        for e in range(r):
            rank = rank + jnp.where(routes[e] == routes[r], 1, 0)
        ranks.append(rank)
    return routes, ranks


def pack_queries(groups, splits, routes_ref, q_ref, out_ref, rows_ref, x_ref, sending):
    requests = q_ref.shape[0]
    routes, ranks = slots_of(routes_ref, requests)
    q = q_ref[...].astype(jnp.float32)
    for k in range(KVH):
        for h in range(PER):
            x_ref[h * requests:(h + 1) * requests, k * HEAD:(k + 1) * HEAD] = q[
                :, (k * PER + h) * HEAD:(k * PER + h + 1) * HEAD
            ]
    x = x_ref[...].astype(jnp.bfloat16)
    cols = PER * requests
    total = groups * ROWS
    row = lax.broadcasted_iota(jnp.int32, (total, cols), 0)
    col = lax.broadcasted_iota(jnp.int32, (total, cols), 1)
    wanted = jnp.full((total, cols), -1, jnp.int32)
    for r in range(requests):
        wanted = jnp.where(col % requests == r, routes[r] * CAP + ranks[r], wanted)
    pick = (row // PER == wanted) & (row % PER == col // requests)
    placed = jnp.dot(
        pick.astype(jnp.float32).astype(jnp.bfloat16), x, preferred_element_type=jnp.float32
    ).astype(jnp.bfloat16)
    for g in range(groups):
        for k in range(KVH):
            tile = placed[g * ROWS:(g + 1) * ROWS, k * HEAD:(k + 1) * HEAD]
            for t in range(splits):
                out_ref[position(g, t * KVH + k, groups, splits * KVH)] = tile
    sending.start()
    mine = requests * PER
    row = lax.broadcasted_iota(jnp.int32, (mine, cols), 0)
    col = lax.broadcasted_iota(jnp.int32, (mine, cols), 1)
    turn = (row // PER == col % requests) & (row % PER == col // requests)
    turned = jnp.dot(
        turn.astype(jnp.float32).astype(jnp.bfloat16), x, preferred_element_type=jnp.float32
    )
    for r in range(requests):
        for k in range(KVH):
            rows_ref[r, k * PER:(k + 1) * PER, :] = turned[
                r * PER:(r + 1) * PER, k * HEAD:(k + 1) * HEAD
            ]


def prepare(groups, splits, routes_in, q_in, kv_ref, out_hbm, rows_ref, routes_ref, *refs):
    blocks, (q_ref, x_ref, out_ref, sems) = refs[:5], refs[5:]
    mine = lax.axis_index("seq") % KVH
    first = [
        pltpu.make_async_copy(routes_in, routes_ref, sems.at[KVH]),
        pltpu.make_async_copy(q_in, q_ref, sems.at[KVH + 1]),
    ]
    later = []
    for j in range(KVH):
        start = pl.multiple_of(jnp.bitwise_xor(mine, j) * HEAD, HEAD)
        later.append(
            pltpu.make_async_copy(
                kv_ref.at[0, :, :, pl.ds(start, HEAD)],
                blocks[j] if j < 2 else blocks[1 + j // 2].at[j % 2],
                sems.at[j],
            )
        )
    for copy in first + later:
        copy.start()
    for copy in first:
        copy.wait()
    sending = pltpu.make_async_copy(out_ref, out_hbm, sems.at[KVH + 2])
    pack_queries(groups, splits, routes_ref, q_ref, out_ref, rows_ref, x_ref, sending)
    for copy in later:
        copy.wait()
    sending.wait()


def suffix_kernel(len_in, rows_ref, new_in, kv_in, out_ref, stat_ref, len_ref, new_ref, kv_ref, sems):
    requests = rows_ref.shape[0]
    small = [
        pltpu.make_async_copy(len_in, len_ref, sems.at[2 * requests]),
        pltpu.make_async_copy(new_in, new_ref, sems.at[2 * requests + 1]),
    ]
    cached = [
        [
            pltpu.make_async_copy(kv_in.at[r, j], kv_ref.at[r, j], sems.at[2 * r + j])
            for r in range(requests)
        ]
        for j in range(2)
    ]
    for copy in small + cached[0] + cached[1]:
        copy.start()
    upper = lax.broadcasted_iota(jnp.int32, (2 * PER, HEAD), 0) < PER
    wides = []
    for r in range(requests):
        q = rows_ref[r]
        wides.append([])
        for pair in range(KVH // 2):
            two = q[2 * pair * PER:2 * (pair + 1) * PER]
            wides[r].append(
                jnp.concatenate(
                    [jnp.where(upper, two, 0.0), jnp.where(upper, 0.0, two)], axis=1
                ).astype(jnp.bfloat16)
            )
    for copy in small:
        copy.wait()
    news, owns, raws = [], [], []
    for r in range(requests):
        q = rows_ref[r]
        new = new_ref[r].astype(jnp.float32)
        news.append(new)
        owns.append(
            jnp.concatenate(
                [
                    jnp.sum(
                        q[k * PER:(k + 1) * PER] * new[0:1, k * HEAD:(k + 1) * HEAD],
                        axis=1,
                        keepdims=True,
                    )
                    for k in range(KVH)
                ],
                axis=0,
            )
        )
    for r in range(requests):
        cached[0][r].wait()
        raw = jnp.concatenate(
            [
                lax.dot_general(
                    wides[r][pair],
                    kv_ref[r, 0, :, 2 * pair * HEAD:2 * (pair + 1) * HEAD],
                    NT,
                    preferred_element_type=jnp.float32,
                )
                for pair in range(KVH // 2)
            ],
            axis=0,
        )
        live = lax.broadcasted_iota(jnp.int32, raw.shape, 1) < len_ref[r]
        raws.append(jnp.where(live, raw, -jnp.inf))
    weights, own_weights, shares = [], [], []
    for r in range(requests):
        top = jnp.maximum(jnp.max(raws[r], axis=1, keepdims=True), owns[r])
        weight = jnp.exp2((raws[r] - top) * (SCALE * LOG2E))
        own_weight = jnp.exp2((owns[r] - top) * (SCALE * LOG2E))
        total = jnp.sum(weight, axis=1, keepdims=True) + own_weight
        stat_ref[r] = jnp.broadcast_to(top * SCALE + jnp.log(total), (HEADS, HEAD))
        shares.append(1.0 / total)
        weights.append(weight.astype(jnp.bfloat16))
        own_weights.append(own_weight.astype(jnp.bfloat16).astype(jnp.float32))
    for r in range(requests):
        cached[1][r].wait()
        for pair in range(KVH // 2):
            both = jnp.dot(
                weights[r][2 * pair * PER:2 * (pair + 1) * PER],
                kv_ref[r, 1, :, 2 * pair * HEAD:2 * (pair + 1) * HEAD],
                preferred_element_type=jnp.float32,
            )
            for j in range(2):
                k = 2 * pair + j
                rows = slice(k * PER, (k + 1) * PER)
                cols = slice(k * HEAD, (k + 1) * HEAD)
                out_ref[r, rows, :] = shares[r][rows] * (
                    both[j * PER:(j + 1) * PER, j * HEAD:(j + 1) * HEAD]
                    + own_weights[r][rows] * news[r][1:2, cols]
                )


def prefix_kernel(splits, q_ref, *refs):
    parts, out_ref = refs[:-1], refs[-1]
    send = out_ref.dtype
    views = [part for part in parts[:2]]
    views += [part.at[0] for part in parts[2:5]] + [part.at[1] for part in parts[5:]]
    keys = jnp.concatenate([view[0] for view in views], axis=0)
    values = jnp.concatenate([view[1] for view in views], axis=0)
    sources = q_ref.shape[0]
    step = HEAD // ROWS
    shape = (step * ROWS, HEAD)
    diagonal = lax.broadcasted_iota(jnp.int32, shape, 0) == lax.broadcasted_iota(jnp.int32, shape, 1)
    low = lax.broadcasted_iota(jnp.int32, (1, HEAD), 1) < HALF

    def score(i):
        q = q_ref[pl.ds(i * step, step)].reshape(shape)
        return lax.dot_general(q, keys, NT, preferred_element_type=jnp.float32)

    def weigh(raw):
        top = jnp.max(raw, axis=1, keepdims=True)
        weight = jnp.exp2((raw - top) * (SCALE * LOG2E))
        total = jnp.sum(weight, axis=1, keepdims=True)
        rounded = weight.astype(jnp.bfloat16)
        if splits == 1:
            return top, (rounded,), total
        return top, (rounded, (weight - rounded.astype(jnp.float32)).astype(jnp.bfloat16)), total

    def store(i, top, weights, total):
        out = sum(jnp.dot(w, values, preferred_element_type=jnp.float32) for w in weights)
        out = (out / total).astype(send)
        level = top * SCALE + jnp.log(total)
        level = jnp.sum(jnp.where(diagonal, level, 0.0), axis=0, keepdims=True)
        first = level.astype(send).astype(jnp.float32)
        rest = level - first
        second = rest.astype(send).astype(jnp.float32)
        third = rest - second
        turned = [pltpu.roll(piece, HALF, 1) for piece in (first, second, third)]
        halves = [
            jnp.concatenate([jnp.where(low, first, turned[1]), third], axis=0).astype(send),
            jnp.concatenate([jnp.where(low, turned[0], second), turned[2]], axis=0).astype(send),
        ]
        for s in range(step):
            at = (i * step + s) * BACK
            out_ref[pl.ds(at, PAIRS)] = out[s * ROWS:(s + 1) * ROWS].reshape(PAIRS, 2, HEAD)
            out_ref[at + PAIRS] = halves[s // (step // 2)]

    def several(start, count):
        ahead, done = score(start), None
        for i in range(count):
            raw = ahead
            if i + 1 < count:
                ahead = score(start + i + 1)
            ready = weigh(raw)
            if done is not None:
                store(start + i - 1, *done)
            done = ready
        store(start + count - 1, *done)

    blocks = sources // step
    count = 4 if blocks % 4 == 0 else 1
    if blocks == count:
        several(0, count)
    else:
        lax.fori_loop(0, blocks // count, lambda i, c: (several(i * count, count), c)[1], 0)


def join_kernel(splits, routes_ref, back_ref, suffix_ref, stat_ref, out_ref):
    requests = out_ref.shape[0]
    routes, ranks = slots_of(routes_ref, requests)
    step = HEAD // ROWS // 2
    place = position(lax.axis_index("grp"), lax.axis_index("seq"), lax.axis_size("grp"), lax.axis_size("seq")) % step * ROWS
    lane = lax.broadcasted_iota(jnp.int32, (PER, HEAD), 1)
    head = lax.broadcasted_iota(jnp.int32, (PER, HEAD), 0)
    pieces = [[None] * requests for _ in range(KVH)]
    for r in range(requests):
        stats = stat_ref[r]
        once = lane == head + (place + ranks[r] * PER)
        twice = lane % HALF == head + (place + ranks[r] * PER)
        for k in range(KVH):
            rows = slice(k * PER, (k + 1) * PER)
            levels, parts = [], []
            for t in range(splits):
                at = position(routes[r], t * KVH + k, lax.axis_size("grp"), splits * KVH) * BACK
                pair = back_ref[pl.ds(at + ranks[r] * (PER // 2), PER // 2)]
                parts.append(pair.reshape(PER, HEAD).astype(jnp.float32))
                stat = back_ref[at + PAIRS].astype(jnp.float32)
                stat = jnp.where(twice, stat[0:1], 0.0) + jnp.where(once, stat[1:2], 0.0)
                levels.append(jnp.sum(stat, axis=1, keepdims=True))
            base = stats[rows, :]
            mixed = suffix_ref[r, rows, :]
            if splits == 1:
                ahead = levels[0] - base
                less = jnp.exp(-jnp.abs(ahead))
                more = 1.0 / (1.0 + less)
                less = less * more
                pieces[k][r] = (
                    jnp.where(ahead >= 0.0, more, less) * parts[0]
                    + jnp.where(ahead >= 0.0, less, more) * mixed
                )
                continue
            top = base
            for level in levels:
                top = jnp.maximum(top, level)
            denom = jnp.exp(base - top)
            numer = denom * mixed
            for level, part in zip(levels, parts):
                from_prefix = jnp.exp(level - top)
                numer = numer + from_prefix * part
                denom = denom + from_prefix
            pieces[k][r] = numer / denom
    stacked = jnp.concatenate(
        [jnp.concatenate(pieces[k], axis=0) for k in range(KVH)], axis=1
    ).astype(jnp.bfloat16)
    mine = requests * PER
    row = lax.broadcasted_iota(jnp.int32, (PER * 8, mine), 0)
    col = lax.broadcasted_iota(jnp.int32, (PER * 8, mine), 1)
    turn = (row % 8 == col // PER) & (row // 8 == col % PER)
    turned = jnp.dot(
        turn.astype(jnp.float32).astype(jnp.bfloat16), stacked, preferred_element_type=jnp.float32
    ).astype(jnp.bfloat16)
    turned = turned.astype(jnp.float32)
    for k in range(KVH):
        for h in range(PER):
            out_ref[:, (k * PER + h) * HEAD:(k * PER + h + 1) * HEAD] = turned[
                h * 8:h * 8 + requests, k * HEAD:(k + 1) * HEAD
            ].astype(jnp.bfloat16)


def on_device(queries, new_kv, suffix_kv, suffix_len, prefix_of, prefix_kv):
    groups = lax.axis_size("grp")
    seq = lax.axis_size("seq")
    splits = seq // KVH
    requests = queries.shape[0]
    span = suffix_kv.shape[2]
    here = prefix_kv.shape[2]
    everyone = ("grp", "seq")
    order = [0] * (groups * seq)
    for g in range(groups):
        for s in range(seq):
            order[position(g, s, groups, seq)] = g * seq + s
    routes = prefix_of.reshape(requests)

    outgoing, rows, routes, *blocks = pl.pallas_call(
        functools.partial(prepare, groups, splits),
        out_shape=[
            jax.ShapeDtypeStruct((groups * seq, ROWS, HEAD), jnp.bfloat16),
            pltpu.VMEM((requests, HEADS, HEAD), jnp.float32),
            pltpu.SMEM((requests,), jnp.int32),
        ]
        + [pltpu.VMEM((2, here, HEAD), jnp.bfloat16)] * 2
        + [pltpu.VMEM((2, 2, here, HEAD), jnp.bfloat16)] * 3,
        in_specs=[ANY, ANY, ANY],
        out_specs=[ANY, VMEM, SMEM] + [VMEM] * 5,
        scratch_shapes=[
            pltpu.VMEM((requests, HEADS * HEAD), jnp.bfloat16),
            pltpu.VMEM((PER * requests, KVH * HEAD), jnp.float32),
            pltpu.VMEM((groups * seq, ROWS, HEAD), jnp.bfloat16),
            pltpu.SemaphoreType.DMA((KVH + 3,)),
        ],
        name="prepare",
    )(routes, queries, prefix_kv)
    def swap(block, j):
        return lax.ppermute(block, "seq", [(s, s ^ j) for s in range(seq)])

    parts = [blocks[0], swap(blocks[1], 1)]
    pairs = [swap(blocks[1 + j // 2], j) for j in (6, 4, 2)]
    parts += pairs + [swap(pair, 1) for pair in pairs]

    arrived = lax.all_to_all(
        outgoing, everyone, split_axis=0, concat_axis=0, tiled=True, axis_index_groups=[order]
    )

    suffix_out, suffix_stat = pl.pallas_call(
        suffix_kernel,
        out_shape=(
            pltpu.VMEM((requests, HEADS, HEAD), jnp.float32),
            pltpu.VMEM((requests, HEADS, HEAD), jnp.float32),
        ),
        in_specs=[ANY, VMEM, ANY, ANY],
        out_specs=(VMEM, VMEM),
        scratch_shapes=[
            pltpu.SMEM((requests,), jnp.int32),
            pltpu.VMEM(new_kv.shape, jnp.bfloat16),
            pltpu.VMEM(suffix_kv.shape, jnp.bfloat16),
            pltpu.SemaphoreType.DMA((2 * requests + 2,)),
        ],
        cost_estimate=pl.CostEstimate(
            flops=4 * requests * HEADS * KVH * HEAD * span,
            bytes_accessed=2 * suffix_kv.size,
            transcendentals=requests * HEADS * span,
        ),
        name="suffix_attention",
    )(suffix_len, in_vmem(rows), new_kv, suffix_kv)

    arrived, suffix_out, suffix_stat = lax.optimization_barrier(
        (arrived, suffix_out, suffix_stat)
    )

    send = jnp.bfloat16 if splits == 1 else jnp.float32
    back = pl.pallas_call(
        functools.partial(prefix_kernel, splits),
        out_shape=pltpu.VMEM((groups * seq * BACK, 2, HEAD), send),
        in_specs=[VMEM] * (1 + KVH),
        out_specs=VMEM,
        compiler_params=pltpu.CompilerParams(vmem_limit_bytes=32 * 1024 * 1024),
        name="prefix_attention",
    )(arrived, *parts)

    home = in_vmem(
        lax.all_to_all(
            back, everyone, split_axis=0, concat_axis=0, tiled=True, axis_index_groups=[order]
        )
    )

    return pl.pallas_call(
        functools.partial(join_kernel, splits),
        out_shape=jax.ShapeDtypeStruct((requests, HEADS * HEAD), jnp.bfloat16),
        in_specs=[SMEM, VMEM, VMEM, VMEM],
        out_specs=VMEM,
        name="join",
    )(in_smem(routes), home, in_vmem(suffix_out), in_vmem(suffix_stat))


def solution(mesh):
    in_specs = (
        P(("grp", "seq"), None),
        P(("grp", "seq"), None, None),
        P(("grp", "seq"), None, None, None),
        P(("grp", "seq")),
        P(("grp", "seq"), None),
        P("grp", None, "seq", None),
    )
    out_specs = P(("grp", "seq"), None)
    return jax.shard_map(
        on_device, mesh=mesh, in_specs=in_specs, out_specs=out_specs, check_vma=False
    )
```

```python
import functools
import math

import jax
import jax.numpy as jnp
from jax import lax
from jax.experimental import pallas as pl
from jax.experimental.pallas import tpu as pltpu
from jax.sharding import PartitionSpec as P

HEADS = 64
KVH = 8
HEAD = 128
CAP = 2
PER = HEADS // KVH
SCALE = HEAD ** (-0.5)
LOG2E = math.log2(math.e)
LN2 = math.log(2.0)
ROWS = CAP * PER
PAIRS = ROWS // 2
BACK = PAIRS + 1
HALF = HEAD // 2
NT = (((1,), (1,)), ((), ()))
VMEM = pl.BlockSpec(memory_space=pltpu.VMEM)
SMEM = pl.BlockSpec(memory_space=pltpu.SMEM)
ANY = pl.BlockSpec(memory_space=pl.ANY)
in_smem = functools.partial(pltpu.with_memory_space_constraint, memory_space=pltpu.SMEM)
in_vmem = functools.partial(pltpu.with_memory_space_constraint, memory_space=pltpu.VMEM)


def position(g, s, groups, seq):
    return s * groups + (groups - 1 - g)


def slots_of(routes_ref, requests):
    routes = [routes_ref[r] for r in range(requests)]
    ranks = []
    for r in range(requests):
        rank = jnp.int32(0)
        for e in range(r):
            rank = rank + jnp.where(routes[e] == routes[r], 1, 0)
        ranks.append(rank)
    return routes, ranks


def pack_queries(groups, splits, routes_ref, q_ref, out_ref, rows_ref, x_ref, sending):
    requests = q_ref.shape[0]
    routes, ranks = slots_of(routes_ref, requests)
    q = q_ref[...].astype(jnp.float32)
    for k in range(KVH):
        for h in range(PER):
            x_ref[h * requests:(h + 1) * requests, k * HEAD:(k + 1) * HEAD] = q[
                :, (k * PER + h) * HEAD:(k * PER + h + 1) * HEAD
            ]
    x = x_ref[...].astype(jnp.bfloat16)
    cols = PER * requests
    total = groups * ROWS
    row = lax.broadcasted_iota(jnp.int32, (total, cols), 0)
    col = lax.broadcasted_iota(jnp.int32, (total, cols), 1)
    wanted = jnp.full((total, cols), -1, jnp.int32)
    for r in range(requests):
        wanted = jnp.where(col % requests == r, routes[r] * CAP + ranks[r], wanted)
    pick = (row // PER == wanted) & (row % PER == col // requests)
    placed = jnp.dot(
        pick.astype(jnp.float32).astype(jnp.bfloat16), x, preferred_element_type=jnp.float32
    ).astype(jnp.bfloat16)
    for g in range(groups):
        for k in range(KVH):
            tile = placed[g * ROWS:(g + 1) * ROWS, k * HEAD:(k + 1) * HEAD]
            for t in range(splits):
                out_ref[position(g, t * KVH + k, groups, splits * KVH)] = tile
    sending.start()
    mine = requests * PER
    row = lax.broadcasted_iota(jnp.int32, (mine, cols), 0)
    col = lax.broadcasted_iota(jnp.int32, (mine, cols), 1)
    turn = (row // PER == col % requests) & (row % PER == col // requests)
    turned = jnp.dot(
        turn.astype(jnp.float32).astype(jnp.bfloat16), x, preferred_element_type=jnp.float32
    )
    for r in range(requests):
        for k in range(KVH):
            rows_ref[r, k * PER:(k + 1) * PER, :] = turned[
                r * PER:(r + 1) * PER, k * HEAD:(k + 1) * HEAD
            ]


def prepare(groups, splits, routes_in, q_in, kv_ref, out_hbm, rows_ref, routes_ref, *refs):
    blocks, (q_ref, x_ref, out_ref, sems) = refs[:5], refs[5:]
    mine = lax.axis_index("seq") % KVH
    first = [
        pltpu.make_async_copy(routes_in, routes_ref, sems.at[KVH]),
        pltpu.make_async_copy(q_in, q_ref, sems.at[KVH + 1]),
    ]
    later = []
    for j in range(KVH):
        start = pl.multiple_of(jnp.bitwise_xor(mine, j) * HEAD, HEAD)
        later.append(
            pltpu.make_async_copy(
                kv_ref.at[0, :, :, pl.ds(start, HEAD)],
                blocks[j] if j < 2 else blocks[1 + j // 2].at[j % 2],
                sems.at[j],
            )
        )
    for copy in first + later:
        copy.start()
    for copy in first:
        copy.wait()
    sending = pltpu.make_async_copy(out_ref, out_hbm, sems.at[KVH + 2])
    pack_queries(groups, splits, routes_ref, q_ref, out_ref, rows_ref, x_ref, sending)
    for copy in later:
        copy.wait()
    sending.wait()


def suffix_kernel(len_in, rows_ref, new_in, kv_in, out_ref, stat_ref, len_ref, new_ref, kv_ref, sems):
    requests = rows_ref.shape[0]
    small = [
        pltpu.make_async_copy(len_in, len_ref, sems.at[2 * requests]),
        pltpu.make_async_copy(new_in, new_ref, sems.at[2 * requests + 1]),
    ]
    cached = [
        [
            pltpu.make_async_copy(kv_in.at[r, j], kv_ref.at[r, j], sems.at[2 * r + j])
            for r in range(requests)
        ]
        for j in range(2)
    ]
    for copy in small + cached[0] + cached[1]:
        copy.start()
    upper = lax.broadcasted_iota(jnp.int32, (2 * PER, HEAD), 0) < PER
    wides = []
    for r in range(requests):
        q = rows_ref[r]
        wides.append([])
        for pair in range(KVH // 2):
            two = q[2 * pair * PER:2 * (pair + 1) * PER]
            wides[r].append(
                jnp.concatenate(
                    [jnp.where(upper, two, 0.0), jnp.where(upper, 0.0, two)], axis=1
                ).astype(jnp.bfloat16)
            )
    for copy in small:
        copy.wait()
    news, owns, raws = [], [], []
    for r in range(requests):
        q = rows_ref[r]
        new = new_ref[r].astype(jnp.float32)
        news.append(new)
        owns.append(
            jnp.concatenate(
                [
                    jnp.broadcast_to(
                        jnp.sum(
                            q[k * PER:(k + 1) * PER] * new[0:1, k * HEAD:(k + 1) * HEAD],
                            axis=1,
                            keepdims=True,
                        ),
                        (PER, HEAD),
                    )
                    for k in range(KVH)
                ],
                axis=0,
            )
        )
    for r in range(requests):
        cached[0][r].wait()
        raw = jnp.concatenate(
            [
                lax.dot_general(
                    wides[r][pair],
                    kv_ref[r, 0, :, 2 * pair * HEAD:2 * (pair + 1) * HEAD],
                    NT,
                    preferred_element_type=jnp.float32,
                )
                for pair in range(KVH // 2)
            ],
            axis=0,
        )
        live = lax.broadcasted_iota(jnp.int32, raw.shape, 1) < len_ref[r]
        raws.append(jnp.where(live, raw, -jnp.inf))
    weights, own_weights, shares = [], [], []
    for r in range(requests):
        top = jnp.maximum(jnp.max(raws[r], axis=1, keepdims=True), owns[r])
        weight = jnp.exp2((raws[r] - top[:, :raws[r].shape[1]]) * (SCALE * LOG2E))
        own_weight = jnp.exp2((owns[r] - top) * (SCALE * LOG2E))
        total = jnp.sum(weight, axis=1, keepdims=True) + own_weight
        stat_ref[r] = top * SCALE + jnp.log(total)
        shares.append(1.0 / total)
        weights.append(weight.astype(jnp.bfloat16))
        own_weights.append(own_weight.astype(jnp.bfloat16).astype(jnp.float32))
    for r in range(requests):
        cached[1][r].wait()
        for pair in range(KVH // 2):
            both = jnp.dot(
                weights[r][2 * pair * PER:2 * (pair + 1) * PER],
                kv_ref[r, 1, :, 2 * pair * HEAD:2 * (pair + 1) * HEAD],
                preferred_element_type=jnp.float32,
            )
            for j in range(2):
                k = 2 * pair + j
                rows = slice(k * PER, (k + 1) * PER)
                cols = slice(k * HEAD, (k + 1) * HEAD)
                out_ref[r, rows, :] = shares[r][rows] * (
                    both[j * PER:(j + 1) * PER, j * HEAD:(j + 1) * HEAD]
                    + own_weights[r][rows] * news[r][1:2, cols]
                )


def prefix_kernel(splits, q_ref, *refs):
    parts, out_ref = refs[:-1], refs[-1]
    send = out_ref.dtype
    views = [part for part in parts[:2]]
    views += [part.at[0] for part in parts[2:5]] + [part.at[1] for part in parts[5:]]
    keys = jnp.concatenate([view[0] for view in views], axis=0)
    values = jnp.concatenate([view[1] for view in views], axis=0)
    sources = q_ref.shape[0]
    step = HEAD // ROWS
    shape = (step * ROWS, HEAD)
    diagonal = lax.broadcasted_iota(jnp.int32, shape, 0) == lax.broadcasted_iota(jnp.int32, shape, 1)
    low = lax.broadcasted_iota(jnp.int32, (1, HEAD), 1) < HALF

    def score(i):
        q = q_ref[pl.ds(i * step, step)].reshape(shape)
        return lax.dot_general(q, keys, NT, preferred_element_type=jnp.float32)

    def weigh(raw):
        top = jnp.max(raw, axis=1, keepdims=True)
        weight = jnp.exp2((raw - top) * (SCALE * LOG2E))
        total = jnp.sum(weight, axis=1, keepdims=True)
        rounded = weight.astype(jnp.bfloat16)
        if splits == 1:
            return top, (rounded,), total
        return top, (rounded, (weight - rounded.astype(jnp.float32)).astype(jnp.bfloat16)), total

    def store(i, top, weights, total):
        out = sum(jnp.dot(w, values, preferred_element_type=jnp.float32) for w in weights)
        out = (out / total).astype(send)
        level = top * SCALE + jnp.log(total)
        level = jnp.sum(jnp.where(diagonal, level, 0.0), axis=0, keepdims=True)
        first = level.astype(send).astype(jnp.float32)
        rest = level - first
        second = rest.astype(send).astype(jnp.float32)
        third = rest - second
        turned = [pltpu.roll(piece, HALF, 1) for piece in (first, second, third)]
        halves = [
            jnp.concatenate([jnp.where(low, first, turned[1]), third], axis=0).astype(send),
            jnp.concatenate([jnp.where(low, turned[0], second), turned[2]], axis=0).astype(send),
        ]
        for s in range(step):
            at = (i * step + s) * BACK
            out_ref[pl.ds(at, PAIRS)] = out[s * ROWS:(s + 1) * ROWS].reshape(PAIRS, 2, HEAD)
            out_ref[at + PAIRS] = halves[s // (step // 2)]

    def several(start, count):
        ahead, done = score(start), None
        for i in range(count):
            raw = ahead
            if i + 1 < count:
                ahead = score(start + i + 1)
            ready = weigh(raw)
            if done is not None:
                store(start + i - 1, *done)
            done = ready
        store(start + count - 1, *done)

    blocks = sources // step
    count = 4 if blocks % 4 == 0 else 1
    if blocks == count:
        several(0, count)
    else:
        lax.fori_loop(0, blocks // count, lambda i, c: (several(i * count, count), c)[1], 0)


def join_kernel(splits, routes_ref, back_ref, suffix_ref, stat_ref, out_ref):
    requests = out_ref.shape[0]
    routes, ranks = slots_of(routes_ref, requests)
    step = HEAD // ROWS // 2
    place = position(lax.axis_index("grp"), lax.axis_index("seq"), lax.axis_size("grp"), lax.axis_size("seq")) % step * ROWS
    lane = lax.broadcasted_iota(jnp.int32, (PER, HEAD), 1)
    head = lax.broadcasted_iota(jnp.int32, (PER, HEAD), 0)
    pieces = [[None] * requests for _ in range(KVH)]
    for r in range(requests):
        stats = stat_ref[r]
        once = lane == head + (place + ranks[r] * PER)
        twice = lane % HALF == head + (place + ranks[r] * PER)
        for k in range(KVH):
            rows = slice(k * PER, (k + 1) * PER)
            levels, parts = [], []
            for t in range(splits):
                at = position(routes[r], t * KVH + k, lax.axis_size("grp"), splits * KVH) * BACK
                pair = back_ref[pl.ds(at + ranks[r] * (PER // 2), PER // 2)]
                parts.append(pair.reshape(PER, HEAD).astype(jnp.float32))
                stat = back_ref[at + PAIRS].astype(jnp.float32)
                stat = jnp.where(twice, stat[0:1], 0.0) + jnp.where(once, stat[1:2], 0.0)
                levels.append(jnp.sum(stat, axis=1, keepdims=True))
            base = stats[rows, :]
            mixed = suffix_ref[r, rows, :]
            if splits == 1:
                ahead = levels[0] - base
                less = jnp.exp(-jnp.abs(ahead))
                more = 1.0 / (1.0 + less)
                less = less * more
                pieces[k][r] = (
                    jnp.where(ahead >= 0.0, more, less) * parts[0]
                    + jnp.where(ahead >= 0.0, less, more) * mixed
                )
                continue
            top = base
            for level in levels:
                top = jnp.maximum(top, level)
            denom = jnp.exp(base - top)
            numer = denom * mixed
            for level, part in zip(levels, parts):
                from_prefix = jnp.exp(level - top)
                numer = numer + from_prefix * part
                denom = denom + from_prefix
            pieces[k][r] = numer / denom
    stacked = jnp.concatenate(
        [jnp.concatenate(pieces[k], axis=0) for k in range(KVH)], axis=1
    ).astype(jnp.bfloat16)
    mine = requests * PER
    row = lax.broadcasted_iota(jnp.int32, (PER * 8, mine), 0)
    col = lax.broadcasted_iota(jnp.int32, (PER * 8, mine), 1)
    turn = (row % 8 == col // PER) & (row // 8 == col % PER)
    turned = jnp.dot(
        turn.astype(jnp.float32).astype(jnp.bfloat16), stacked, preferred_element_type=jnp.float32
    ).astype(jnp.bfloat16)
    turned = turned.astype(jnp.float32)
    for k in range(KVH):
        for h in range(PER):
            out_ref[:, (k * PER + h) * HEAD:(k * PER + h + 1) * HEAD] = turned[
                h * 8:h * 8 + requests, k * HEAD:(k + 1) * HEAD
            ].astype(jnp.bfloat16)


def on_device(queries, new_kv, suffix_kv, suffix_len, prefix_of, prefix_kv):
    groups = lax.axis_size("grp")
    seq = lax.axis_size("seq")
    splits = seq // KVH
    requests = queries.shape[0]
    span = suffix_kv.shape[2]
    here = prefix_kv.shape[2]
    everyone = ("grp", "seq")
    order = [0] * (groups * seq)
    for g in range(groups):
        for s in range(seq):
            order[position(g, s, groups, seq)] = g * seq + s
    routes = prefix_of.reshape(requests)

    outgoing, rows, routes, *blocks = pl.pallas_call(
        functools.partial(prepare, groups, splits),
        out_shape=[
            jax.ShapeDtypeStruct((groups * seq, ROWS, HEAD), jnp.bfloat16),
            pltpu.VMEM((requests, HEADS, HEAD), jnp.float32),
            pltpu.SMEM((requests,), jnp.int32),
        ]
        + [pltpu.VMEM((2, here, HEAD), jnp.bfloat16)] * 2
        + [pltpu.VMEM((2, 2, here, HEAD), jnp.bfloat16)] * 3,
        in_specs=[ANY, ANY, ANY],
        out_specs=[ANY, VMEM, SMEM] + [VMEM] * 5,
        scratch_shapes=[
            pltpu.VMEM((requests, HEADS * HEAD), jnp.bfloat16),
            pltpu.VMEM((PER * requests, KVH * HEAD), jnp.float32),
            pltpu.VMEM((groups * seq, ROWS, HEAD), jnp.bfloat16),
            pltpu.SemaphoreType.DMA((KVH + 3,)),
        ],
        name="prepare",
    )(routes, queries, prefix_kv)
    def swap(block, j):
        return lax.ppermute(block, "seq", [(s, s ^ j) for s in range(seq)])

    parts = [blocks[0], swap(blocks[1], 1)]
    pairs = [swap(blocks[1 + j // 2], j) for j in (6, 4, 2)]
    parts += pairs + [swap(pair, 1) for pair in pairs]

    arrived = lax.all_to_all(
        outgoing, everyone, split_axis=0, concat_axis=0, tiled=True, axis_index_groups=[order]
    )

    suffix_out, suffix_stat = pl.pallas_call(
        suffix_kernel,
        out_shape=(
            pltpu.VMEM((requests, HEADS, HEAD), jnp.float32),
            pltpu.VMEM((requests, HEADS, HEAD), jnp.float32),
        ),
        in_specs=[ANY, VMEM, ANY, ANY],
        out_specs=(VMEM, VMEM),
        scratch_shapes=[
            pltpu.SMEM((requests,), jnp.int32),
            pltpu.VMEM(new_kv.shape, jnp.bfloat16),
            pltpu.VMEM(suffix_kv.shape, jnp.bfloat16),
            pltpu.SemaphoreType.DMA((2 * requests + 2,)),
        ],
        cost_estimate=pl.CostEstimate(
            flops=4 * requests * HEADS * KVH * HEAD * span,
            bytes_accessed=2 * suffix_kv.size,
            transcendentals=requests * HEADS * span,
        ),
        name="suffix_attention",
    )(suffix_len, in_vmem(rows), new_kv, suffix_kv)

    arrived, suffix_out, suffix_stat = lax.optimization_barrier(
        (arrived, suffix_out, suffix_stat)
    )

    send = jnp.bfloat16 if splits == 1 else jnp.float32
    back = pl.pallas_call(
        functools.partial(prefix_kernel, splits),
        out_shape=pltpu.VMEM((groups * seq * BACK, 2, HEAD), send),
        in_specs=[VMEM] * (1 + KVH),
        out_specs=VMEM,
        compiler_params=pltpu.CompilerParams(vmem_limit_bytes=32 * 1024 * 1024),
        name="prefix_attention",
    )(arrived, *parts)

    home = in_vmem(
        lax.all_to_all(
            back, everyone, split_axis=0, concat_axis=0, tiled=True, axis_index_groups=[order]
        )
    )

    return pl.pallas_call(
        functools.partial(join_kernel, splits),
        out_shape=jax.ShapeDtypeStruct((requests, HEADS * HEAD), jnp.bfloat16),
        in_specs=[SMEM, VMEM, VMEM, VMEM],
        out_specs=VMEM,
        name="join",
    )(in_smem(routes), home, in_vmem(suffix_out), in_vmem(suffix_stat))


def solution(mesh):
    in_specs = (
        P(("grp", "seq"), None),
        P(("grp", "seq"), None, None),
        P(("grp", "seq"), None, None, None),
        P(("grp", "seq")),
        P(("grp", "seq"), None),
        P("grp", None, "seq", None),
    )
    out_specs = P(("grp", "seq"), None)
    return jax.shard_map(
        on_device, mesh=mesh, in_specs=in_specs, out_specs=out_specs, check_vma=False
    )
```
